32 devices in a mesh: ctx: 8 (over y, x, core), tp: 4 (over z).
Axes of the slice: x: 2, y: 2, z: 4, core: 2. Of those that a mesh axis runs over, the one named last changes fastest.
Arguments:
- tokens: bfloat16 [4096, 2304], P(('ctx', 'tp')), may hold values from -8 to 8
- cotangent: bfloat16 [4096, 2304], P(('ctx', 'tp')), may hold values from -6 to 6
- w_query: bfloat16 [2304, 2048], P('ctx', 'tp'), may hold values from -0.125 to 0.125
- key_projection: bfloat16 [2304, 1024], P('ctx', 'tp'), may hold values from -0.125 to 0.125
- value_projection: bfloat16 [2304, 1024], P('ctx', 'tp'), may hold values from -0.125 to 0.125
- w_out: bfloat16 [2048, 2304], P('tp', 'ctx'), may hold values from -0.125 to 0.125
- w_gate: bfloat16 [2304, 9216], P('ctx', 'tp'), may hold values from -0.125 to 0.125
- w_up: bfloat16 [2304, 9216], P('ctx', 'tp'), may hold values from -0.125 to 0.125
- w_down: bfloat16 [9216, 2304], P('tp', 'ctx'), may hold values from -0.0625 to 0.0625
- norm_gains: bfloat16 [4, 2304], P(None, 'ctx'), may hold values from -0.5 to 0.5
- block_mask: int32 [32, 32], replicated, may hold values from 0 to 1, as said below
- block_seq: int32 [32], replicated, may hold values from 0 to 0, as said below
- block_place: int32 [32], replicated, may hold values from 0 to 31, as said below
Outputs:
- mixed_out: bfloat16 [4096, 2304], P(('ctx', 'tp'))
- grad_tokens: float32 [4096, 2304], P(('ctx', 'tp'))
- grad_query: float32 [2304, 2048], P('ctx', 'tp')
- grad_key: float32 [2304, 1024], P('ctx', 'tp')
- grad_value: float32 [2304, 1024], P('ctx', 'tp')
- grad_out: float32 [2048, 2304], P('tp', 'ctx')
- grad_gate: float32 [2304, 9216], P('ctx', 'tp')
- grad_up: float32 [2304, 9216], P('ctx', 'tp')
- grad_down: float32 [9216, 2304], P('tp', 'ctx')
- grad_gains: float32 [4, 2304], P('tp', 'ctx')
The draws below stay inside these ranges and needn't reach their ends.
Inputs may be any that keep to these rules, and one draw needn't show every extreme that they name: block_mask[i, i] = 1 and block_mask[i, j] = 0 for j > i. `block_seq`: blocks 2m and 2m + 1 belong to one sequence; each sequence owns 32 blocks. `block_place`: blocks 2m and 2m + 1 hold places p and 31 - p; within a sequence each place occurs once.
All inputs are finite; a program needn't handle non-finite values.
Results may differ from the reference program's by a relative error of at most 0.015.
Values may be sent and summed in bfloat16 or wider, within the bound.
No kernel may reach another device: no remote copies, remote signals or barrier semaphores. Data moves between devices by JAX's collectives and lax.ppermute only.
A program may use at most 192 MiB of HBM per device.

```python
import math
import jax
import jax.numpy as jnp
from jax import lax

MODEL_WIDTH = 2304
QUERY_HEADS = 8
KEY_VALUE_HEADS = 4
HEAD_SIZE = 256
FF = 9216
SCORE_SOFT_LIMIT = 50
BLOCK_TOKENS = 128
SEQ = 4096
TOKEN_COUNT = 4096
BLOCK_COUNT = 32
N_CTX = 8


def dealing(key):
    per_seq = SEQ // (2 * BLOCK_TOKENS)
    pair_total = TOKEN_COUNT // (2 * BLOCK_TOKENS)
    chosen = jax.random.randint(jax.random.fold_in(key, 11), (), 0, TOKEN_COUNT // SEQ)
    pair_ids = jnp.arange(pair_total, dtype=jnp.int32)
    owner = pair_ids // per_seq
    place_now = pair_ids % per_seq
    marked = (owner == chosen) & (place_now < 3)
    shuffled = jax.random.permutation(jax.random.fold_in(key, 12), pair_total).astype(jnp.int32)
    order_key = jnp.where(marked, place_now - 3, shuffled)
    pair_list = jnp.argsort(order_key, stable=True).astype(jnp.int32)
    slot_marked = (pair_ids == 0) | (pair_ids == pair_total // 2) | (pair_ids == pair_total - 1)
    slot_key = jnp.where(slot_marked, -1, pair_ids)
    slot_list = jnp.argsort(slot_key, stable=True).astype(jnp.int32)
    dealt = jnp.zeros((pair_total,), jnp.int32).at[slot_list].set(pair_list)
    return (dealt // per_seq, dealt % per_seq)


def draw_block_seq(key, part):
    owners, places = dealing(key)
    return jnp.repeat(owners, 2).astype(jnp.int32)


def draw_block_place(key, part):
    owners, places = dealing(key)
    mirrored = SEQ // BLOCK_TOKENS - 1 - places
    return jnp.stack([places, mirrored], axis=1).reshape(-1).astype(jnp.int32)


def draw_block_mask(key, part):
    key = jax.random.fold_in(key, 5)
    blocks_seq = SEQ // BLOCK_TOKENS
    coin = jax.random.randint(key, (blocks_seq, blocks_seq), 0, 4)
    row_ids = jnp.arange(blocks_seq, dtype=jnp.int32)[:, None]
    col_ids = jnp.arange(blocks_seq, dtype=jnp.int32)[None, :]
    lower = (coin < 3).astype(jnp.int32)
    return jnp.where(row_ids > col_ids, lower, jnp.where(row_ids == col_ids, 1, 0)).astype(jnp.int32)


def draw_tokens(key, part):
    key = jax.random.fold_in(key, 7)
    base_key, row_key, col_key = jax.random.split(key, 3)
    row_scale = jnp.exp(jax.random.uniform(row_key, (TOKEN_COUNT, 1), minval=math.log(0.3), maxval=math.log(3.0)))
    col_scale = jnp.exp(jax.random.uniform(col_key, (1, MODEL_WIDTH), minval=math.log(0.5), maxval=math.log(2.0)))
    base = jax.random.normal(base_key, (TOKEN_COUNT, MODEL_WIDTH))
    return jnp.clip(base * row_scale * col_scale, -8.0, 8.0).astype(jnp.bfloat16)


def steps_of(stream_key, extent, shards, least, top_value):
    factor_of, own = 1.0, jax.random.fold_in(stream_key, 6)
    for axis_at, parts in shards:
        steps = jnp.exp(jax.random.uniform(jax.random.fold_in(own, axis_at), (parts,), jnp.float32, least / len(shards), top_value / len(shards)))
        factor_of = factor_of * jnp.repeat(steps, extent[axis_at] // parts).reshape([-1 if axis == axis_at else 1 for axis in range(len(extent))])
    return factor_of


def gaussian(stream_key, shape, scale, bound, pieces=(), kind=jnp.bfloat16):
    values = scale * jax.random.normal(stream_key, shape, jnp.float32)
    if pieces:
        values = values * steps_of(stream_key, shape, pieces, -0.22, 0.18)
    return jnp.clip(values, -bound, bound).astype(kind)


def setup_inputs(seed: int = 0) -> dict:
    streams_of = jax.random.split(jax.random.key(seed), 14)
    tokens = draw_tokens(jax.random.fold_in(streams_of[13], 71), 0)
    cotangent = gaussian(streams_of[1], (TOKEN_COUNT, MODEL_WIDTH), 1.0, 6.0, ((0, 32),))
    w_query = gaussian(streams_of[2], (MODEL_WIDTH, QUERY_HEADS * HEAD_SIZE), MODEL_WIDTH ** -0.5, 0.125, ((0, 8), (1, 4)))
    key_projection = gaussian(streams_of[3], (MODEL_WIDTH, KEY_VALUE_HEADS * HEAD_SIZE), MODEL_WIDTH ** -0.5, 0.125, ((0, 8), (1, 4)))
    value_projection = gaussian(streams_of[4], (MODEL_WIDTH, KEY_VALUE_HEADS * HEAD_SIZE), MODEL_WIDTH ** -0.5, 0.125, ((0, 8), (1, 4)))
    w_out = gaussian(streams_of[5], (QUERY_HEADS * HEAD_SIZE, MODEL_WIDTH), (QUERY_HEADS * HEAD_SIZE) ** -0.5, 0.125, ((0, 4), (1, 8)))
    w_gate = gaussian(streams_of[6], (MODEL_WIDTH, FF), MODEL_WIDTH ** -0.5, 0.125, ((0, 8), (1, 4)))
    w_up = gaussian(streams_of[7], (MODEL_WIDTH, FF), MODEL_WIDTH ** -0.5, 0.125, ((0, 8), (1, 4)))
    w_down = gaussian(streams_of[8], (FF, MODEL_WIDTH), FF ** -0.5, 0.0625, ((0, 4), (1, 8)))
    norm_gains = jnp.clip(jax.random.uniform(streams_of[9], (4, MODEL_WIDTH), jnp.float32, -0.5, 0.5) * steps_of(streams_of[9], (4, MODEL_WIDTH), ((1, 8),), -0.4, 0.0), -0.5, 0.5).astype(jnp.bfloat16)
    block_mask = draw_block_mask(jax.random.fold_in(streams_of[13], 71), 0)
    block_seq = draw_block_seq(jax.random.fold_in(streams_of[13], 71), 0)
    block_place = draw_block_place(jax.random.fold_in(streams_of[13], 71), 0)
    return dict(tokens=tokens, cotangent=cotangent, w_query=w_query, key_projection=key_projection, value_projection=value_projection, w_out=w_out, w_gate=w_gate, w_up=w_up, w_down=w_down, norm_gains=norm_gains, block_mask=block_mask, block_seq=block_seq, block_place=block_place)


EPSILON = 1e-06
PRECISE = lax.Precision.HIGHEST

@jax.custom_vjp
def low(v):
    return lax.optimization_barrier(v.astype(jnp.bfloat16)).astype(jnp.float32)

@jax.custom_vjp
def low_back(v):
    return v

def low_keep(v):
    return (low(v), None)

def low_pass(kept, grad):
    return (grad,)

def back_keep(v):
    return (v, None)

def back_low(kept, grad):
    return (low(grad),)
low.defvjp(low_keep, low_pass)
low_back.defvjp(back_keep, back_low)

def matmul_high(first_op, second_op):
    return jnp.dot(first_op, second_op, precision=PRECISE, preferred_element_type=jnp.float32)

def rms_norm(inputs, gain_row):
    inv_rms = lax.rsqrt(lax.optimization_barrier(jnp.mean(inputs * inputs, axis=-1, keepdims=True)) + EPSILON)
    return inputs * inv_rms * (1.0 + gain_row)

def attention(query_matrix, projected_keys, projected_values, block_mask, block_seq, block_place):
    count_of_rows = TOKEN_COUNT // N_CTX
    query_block_rows = count_of_rows // BLOCK_TOKENS
    heads_per_group = QUERY_HEADS // KEY_VALUE_HEADS
    query_matrix = query_matrix.reshape(N_CTX, count_of_rows, KEY_VALUE_HEADS, heads_per_group, HEAD_SIZE)
    projected_keys = projected_keys.reshape(TOKEN_COUNT, KEY_VALUE_HEADS, HEAD_SIZE)
    projected_values = projected_values.reshape(TOKEN_COUNT, KEY_VALUE_HEADS, HEAD_SIZE)
    key_hits = block_mask[:, block_place]

    def one_block(operands):
        query_rows, index_now = operands
        first_block = index_now * query_block_rows
        query_seq = lax.dynamic_slice_in_dim(block_seq, first_block, query_block_rows)
        query_place = lax.dynamic_slice_in_dim(block_place, first_block, query_block_rows)
        permitted_pairs = (query_seq[:, None] == block_seq[None, :]) & (key_hits[query_place] == 1)
        scores = jnp.einsum('qcgd,kcd->cgqk', query_rows, projected_keys, precision=PRECISE)
        scores = low_back(scores)
        incoming_gradient = jnp.tanh(scores / SCORE_SOFT_LIMIT)
        widened_heads = jnp.exp(SCORE_SOFT_LIMIT * incoming_gradient).reshape(KEY_VALUE_HEADS, heads_per_group, query_block_rows, BLOCK_TOKENS, BLOCK_COUNT, BLOCK_TOKENS)
        exponent_weights = jnp.where(permitted_pairs[:, None, :, None], widened_heads, 0.0).reshape(KEY_VALUE_HEADS, heads_per_group, count_of_rows, TOKEN_COUNT)
        totals = lax.optimization_barrier(jnp.sum(exponent_weights, axis=-1))
        summed = jnp.einsum('cgqk,kcd->qcgd', low(exponent_weights), projected_values, precision=PRECISE)
        return low_back(summed) / jnp.transpose(totals, (2, 0, 1))[..., None]
    outcome = lax.map(jax.checkpoint(one_block), (query_matrix, jnp.arange(N_CTX, dtype=jnp.int32)))
    return outcome.reshape(TOKEN_COUNT, QUERY_HEADS * HEAD_SIZE)

def layer(token_rows, w_query, key_projection, value_projection, w_out, w_gate, w_up, w_down, gain_set, block_mask, block_seq, block_place):
    normed = low(rms_norm(token_rows, gain_set[0]))
    query_matrix = low_back(low(matmul_high(normed, w_query) * HEAD_SIZE ** (-0.5)))
    projected_keys = low_back(low(matmul_high(normed, key_projection)))
    projected_values = low_back(low(matmul_high(normed, value_projection)))
    attended = low_back(low(attention(query_matrix, projected_keys, projected_values, block_mask, block_seq, block_place)))
    branch = low_back(matmul_high(attended, w_out))
    hidden = token_rows + rms_norm(branch, gain_set[1])
    inner = low(rms_norm(hidden, gain_set[2]))
    gate_pre = low_back(matmul_high(inner, w_gate))
    up_pre = low_back(matmul_high(inner, w_up))
    mid_rows = low(jax.nn.gelu(gate_pre, approximate=True) * up_pre)
    feed_sum = low_back(matmul_high(mid_rows, w_down))
    return hidden + rms_norm(feed_sum, gain_set[3])

def reference(tokens, cotangent, w_query, key_projection, value_projection, w_out, w_gate, w_up, w_down, norm_gains, block_mask, block_seq, block_place):
    floats = (tokens, w_query, key_projection, value_projection, w_out, w_gate, w_up, w_down, norm_gains)
    floats = tuple((entry.astype(jnp.float32) for entry in floats))

    def forward(token_rows, query_w, key_w, value_w, out_w, gate_w, up_w, down_w, gain_set):
        return layer(token_rows, query_w, key_w, value_w, out_w, gate_w, up_w, down_w, gain_set, block_mask, block_seq, block_place)
    result, pull_back = jax.vjp(forward, *floats)
    grads = pull_back(cotangent.astype(jnp.float32))
    return (result.astype(jnp.bfloat16), grads[0], grads[1], grads[2], grads[3], grads[4], grads[5], grads[6], grads[7], grads[8])
```

```python
import functools

import jax
import jax.numpy as jnp
from jax import lax
from jax.experimental import pallas as pl
from jax.experimental.pallas import tpu as pltpu
from jax.sharding import PartitionSpec as P

QUERY_HEADS = 8
KEY_VALUE_HEADS = 4
HEAD_SIZE = 256
SCORE_SOFT_LIMIT = 50
BLOCK_TOKENS = 128
EPSILON = 1e-06
KEY_STEP = 4

F32 = jnp.float32
BF16 = jnp.bfloat16


def dot(a, b):
    return jnp.dot(a, b, preferred_element_type=F32)


def dot_back(a, b):
    return lax.dot_general(a, b, (((1,), (1,)), ((), ())), preferred_element_type=F32)


def dot_rows(a, b):
    return lax.dot_general(a, b, (((0,), (0,)), ((), ())), preferred_element_type=F32)


def inv_rms(v):
    return lax.rsqrt(jnp.mean(v * v, axis=-1, keepdims=True) + EPSILON)


def norm_input_grad(v, s, gain, c):
    cw = c * gain
    return s * cw - v * (s * s * s) * jnp.mean(cw * v, axis=-1, keepdims=True)


def swap(x, bit):
    size = lax.axis_size("ctx")
    return lax.ppermute(x, "ctx", [(i, i ^ (1 << bit)) for i in range(size)])


def ctx_bits():
    size = lax.axis_size("ctx")
    bits = size.bit_length() - 1
    assert size == 1 << bits and bits >= 1
    return bits


def rel_of(place):
    half = lax.axis_size("ctx") // 2
    return (place % half) * 2 + place // half


def gather_half(x, order):
    held = {0: x}
    for bit in order:
        held |= {rel ^ (1 << bit): swap(held[rel], bit) for rel in list(held)}
    return [held[rel_of(p)] for p in range(lax.axis_size("ctx"))]


def gather_ctx(a, b):
    outer = list(range(1, ctx_bits()))
    return gather_half(a, outer + [0]), gather_half(b, outer[::-1] + [0])


def gather_rows(w):
    half = w.shape[0] // 32 * 16
    a, b = gather_ctx(w[:half], w[half:])
    return jnp.concatenate([piece for pair in zip(a, b) for piece in pair], axis=0)


def scatter_half(sent, kept, order):
    got = swap(sent.astype(BF16), 0)
    now = {r: kept[r].astype(F32) + got[r].astype(F32) for r in range(kept.shape[0])}
    for bit in order:
        mask = 1 << (bit - 1)
        came = {r: swap(v.astype(BF16), bit) for r, v in now.items() if r & mask}
        now = {r: v + came[r | mask].astype(F32) for r, v in now.items() if not r & mask}
    return now[0]


def scatter_pair(sent_a, kept_a, sent_b, kept_b):
    outer = list(range(1, ctx_bits()))
    return scatter_half(sent_a, kept_a, outer[::-1]), scatter_half(sent_b, kept_b, outer)


def scatter_grad(left, right):
    size = lax.axis_size("ctx")
    width = left.shape[1] // 2
    cut = right.shape[1] // 2
    parts = []
    for columns in (right[:, :cut], right[:, cut:]):
        for rows in (left[:, width:], left[:, :width]):
            part = dot_rows(rows, columns).astype(BF16)
            parts.append(part.reshape(size // 2, 2 * width // size, cut))
    return jnp.concatenate(scatter_pair(*parts), axis=1)


def line(x, perm):
    return lax.ppermute(x, "tp", perm)


def gather_tp(x):
    size, me = lax.axis_size("tp"), lax.axis_index("tp")
    up, down = x, x
    ups, downs = {}, {}
    for s in range(1, size):
        up = line(up, [(i, i + 1) for i in range(s - 1, size - 1)])
        down = line(down, [(i, i - 1) for i in range(1, size - s + 1)])
        ups[s], downs[s] = up, down
    rest = [jnp.where(me + r < size, downs[r], ups[size - r]) for r in range(1, size)]
    return jnp.concatenate([x] + rest, axis=0)


def scatter_tp(part):
    size = lax.axis_size("tp")
    rows = part.shape[0] // size
    block = [part[r * rows : (r + 1) * rows] for r in range(size)]
    up = down = 0.0
    for s in range(1, size):
        up_send = (block[size - s].astype(F32) + up).astype(BF16)
        down_send = (block[s].astype(F32) + down).astype(BF16)
        up = line(up_send, [(i, i + 1) for i in range(s)]).astype(F32)
        down = line(down_send, [(i, i - 1) for i in range(size - s, size)]).astype(F32)
    return block[0].astype(F32) + up + down


def take_blocks(ref, index_ref, query_block, step, blocks):
    places = [index_ref[query_block, step * KEY_STEP + j] for j in range(KEY_STEP)]
    starts = [pl.multiple_of(p * BLOCK_TOKENS, BLOCK_TOKENS) for p in places]
    return starts, jnp.concatenate([ref[pl.ds(s, BLOCK_TOKENS), :] for s in starts], axis=0)


def stack_heads(x):
    heads = x.shape[1] // HEAD_SIZE
    return jnp.concatenate([x[:, h * HEAD_SIZE : (h + 1) * HEAD_SIZE] for h in range(heads)], axis=0)


def unstack_heads(x):
    rows = BLOCK_TOKENS
    return jnp.concatenate([x[h * rows : (h + 1) * rows] for h in range(x.shape[0] // rows)], axis=1)


def attend_kernel(index_ref, count_ref, q_ref, k_ref, v_ref, out_ref, total_ref, acc_ref):
    i = pl.program_id(0)
    count = count_ref[i]
    q = stack_heads(q_ref[...])
    acc_ref[...] = jnp.zeros_like(acc_ref)
    total_ref[...] = jnp.zeros_like(total_ref)

    def body(step, carry):
        starts, keys = take_blocks(k_ref, index_ref, i, step, KEY_STEP)
        values = jnp.concatenate([v_ref[pl.ds(s, BLOCK_TOKENS), :] for s in starts], axis=0)
        scores = dot_back(q, keys)
        grown = jnp.exp(SCORE_SOFT_LIMIT * jnp.tanh(scores * (1.0 / SCORE_SOFT_LIMIT)))
        pieces = []
        for j in range(KEY_STEP):
            seen = (step * KEY_STEP + j) < count
            piece = grown[:, j * BLOCK_TOKENS : (j + 1) * BLOCK_TOKENS]
            pieces.append(jnp.where(seen, piece, 0.0))
        total_ref[...] += functools.reduce(jnp.add, pieces)
        acc_ref[...] += dot(jnp.concatenate(pieces, axis=1).astype(BF16), values)
        return carry

    lax.fori_loop(0, (count + KEY_STEP - 1) // KEY_STEP, body, 0)
    totals = jnp.sum(total_ref[...], axis=1, keepdims=True)
    total_ref[...] = jnp.broadcast_to(totals, total_ref.shape)
    out_ref[...] = unstack_heads(acc_ref[...] / totals)


def attend_back_kernel(
    index_ref, count_ref, q_ref, dout_ref, out_ref, total_ref, k_ref, v_ref, dq_ref, dk_ref, dv_ref, acc_ref
):
    i = pl.program_id(0)

    @pl.when(i == 0)
    def _():
        dk_ref[...] = jnp.zeros_like(dk_ref)
        dv_ref[...] = jnp.zeros_like(dv_ref)

    count = count_ref[i]
    q = stack_heads(q_ref[...])
    dout = stack_heads(dout_ref[...]).astype(F32)
    inverse = 1.0 / total_ref[:, :1]
    scaled = (dout * inverse).astype(BF16)
    weighted = dout * stack_heads(out_ref[...]) * inverse
    ones = jnp.ones((8, HEAD_SIZE), F32)
    dtotal = -lax.dot_general(
        ones, weighted, (((1,), (1,)), ((), ())), precision=lax.Precision.HIGHEST, preferred_element_type=F32
    )[:1]
    acc_ref[...] = jnp.zeros_like(acc_ref)

    def body(step, carry):
        starts, keys = take_blocks(k_ref, index_ref, i, step, KEY_STEP)
        values = jnp.concatenate([v_ref[pl.ds(s, BLOCK_TOKENS), :] for s in starts], axis=0)
        soft = jnp.tanh(dot_back(keys, q) * (1.0 / SCORE_SOFT_LIMIT))
        grown = jnp.exp(SCORE_SOFT_LIMIT * soft)
        pieces = []
        for j in range(KEY_STEP):
            seen = (step * KEY_STEP + j) < count
            piece = grown[j * BLOCK_TOKENS : (j + 1) * BLOCK_TOKENS]
            pieces.append(jnp.where(seen, piece, 0.0))
        grown = jnp.concatenate(pieces, axis=0)
        dprob = dot_back(values, scaled)
        dscores = (grown * (dprob + dtotal) * (1.0 - soft * soft)).astype(BF16)
        acc_ref[...] += dot_rows(dscores, keys)
        dkeys = dot(dscores, q)
        dvalues = dot(grown.astype(BF16), scaled)
        for j in range(KEY_STEP):
            at = pl.ds(starts[j], BLOCK_TOKENS)
            dk_ref[at, :] += dkeys[j * BLOCK_TOKENS : (j + 1) * BLOCK_TOKENS]
            dv_ref[at, :] += dvalues[j * BLOCK_TOKENS : (j + 1) * BLOCK_TOKENS]
        return carry

    lax.fori_loop(0, (count + KEY_STEP - 1) // KEY_STEP, body, 0)
    dq_ref[...] = unstack_heads(acc_ref[...]).astype(BF16)


VMEM_LIMIT = 56 * 1024 * 1024


def whole_spec(shape):
    return pl.BlockSpec(shape, lambda i, *_: (0,) * len(shape), pipeline_mode=pl.Buffered(1))


def row_spec(rows, columns):
    return pl.BlockSpec((rows, columns), lambda i, *_: (i, 0))


def attend(index, count, q, k, v):
    rows, columns = q.shape
    blocks, stacked = rows // BLOCK_TOKENS, BLOCK_TOKENS * (columns // HEAD_SIZE)
    return pl.pallas_call(
        attend_kernel,
        grid_spec=pltpu.PrefetchScalarGridSpec(
            num_scalar_prefetch=2,
            grid=(blocks,),
            in_specs=[row_spec(BLOCK_TOKENS, columns), whole_spec(k.shape), whole_spec(v.shape)],
            out_specs=[row_spec(BLOCK_TOKENS, columns), row_spec(stacked, BLOCK_TOKENS)],
            scratch_shapes=[pltpu.VMEM((stacked, HEAD_SIZE), F32)],
        ),
        out_shape=[
            jax.ShapeDtypeStruct((rows, columns), F32),
            jax.ShapeDtypeStruct((blocks * stacked, BLOCK_TOKENS), F32),
        ],
        compiler_params=pltpu.CompilerParams(vmem_limit_bytes=VMEM_LIMIT),
        cost_estimate=pl.CostEstimate(flops=2 * rows * columns * k.shape[0], bytes_accessed=6 << 20, transcendentals=0),
    )(index, count, q, k, v)


def attend_back(index, count, q, dout, out, totals, k, v):
    rows, columns = q.shape
    blocks, stacked = rows // BLOCK_TOKENS, BLOCK_TOKENS * (columns // HEAD_SIZE)
    row = row_spec(BLOCK_TOKENS, columns)
    return pl.pallas_call(
        attend_back_kernel,
        grid_spec=pltpu.PrefetchScalarGridSpec(
            num_scalar_prefetch=2,
            grid=(blocks,),
            in_specs=[row, row, row, row_spec(stacked, BLOCK_TOKENS), whole_spec(k.shape), whole_spec(v.shape)],
            out_specs=[row, whole_spec(k.shape), whole_spec(v.shape)],
            scratch_shapes=[pltpu.VMEM((stacked, HEAD_SIZE), F32)],
        ),
        out_shape=[
            jax.ShapeDtypeStruct((rows, columns), BF16),
            jax.ShapeDtypeStruct(k.shape, F32),
            jax.ShapeDtypeStruct(v.shape, F32),
        ],
        compiler_params=pltpu.CompilerParams(vmem_limit_bytes=VMEM_LIMIT),
        cost_estimate=pl.CostEstimate(flops=5 * rows * columns * k.shape[0], bytes_accessed=16 << 20, transcendentals=0),
    )(index, count, q, dout, out, totals, k, v)


def visible_lists(block_mask, block_seq, block_place, per_device):
    size, tp = lax.axis_size("ctx"), lax.axis_size("tp")
    ctx, me = lax.axis_index("ctx"), lax.axis_index("tp")
    total = block_seq.shape[0]
    turned = (me + jnp.arange(tp, dtype=jnp.int32)) % tp
    inner = (turned[:, None] * per_device + jnp.arange(per_device, dtype=jnp.int32)[None, :]).reshape(-1)
    owner = ctx ^ jnp.array([rel_of(p) for p in range(size)], jnp.int32)
    of_group = tp * per_device
    query_ids = ctx * of_group + inner
    key_ids = (owner[:, None] * of_group + inner[None, :]).reshape(-1)
    every = jnp.arange(total, dtype=jnp.int32)

    def look_up(ids, table):
        return jnp.sum(jnp.where(ids[:, None] == every[None, :], table[None, :], 0), axis=1)

    places = jnp.arange(block_mask.shape[0], dtype=jnp.int32)
    query_pick = (look_up(query_ids, block_place)[:, None] == places[None, :]).astype(F32)
    key_pick = (look_up(key_ids, block_place)[:, None] == places[None, :]).astype(F32)
    hits = dot_back(dot(query_pick, block_mask.astype(F32)), key_pick)
    same = look_up(query_ids, block_seq)[:, None] == look_up(key_ids, block_seq)[None, :]
    seen = (hits > 0.5) & same
    before = (every[:, None] < every[None, :]).astype(F32)
    rank = dot(seen.astype(F32), before).astype(jnp.int32)
    wanted = seen[:, None, :] & (rank[:, None, :] == every[None, :, None])
    index = jnp.sum(jnp.where(wanted, every[None, None, :], 0), axis=2)
    index = jnp.pad(index, ((0, 0), (0, KEY_STEP)))
    return index, jnp.sum(seen.astype(jnp.int32), axis=1)


def to_places(x):
    size, ctx = lax.axis_size("ctx"), lax.axis_index("ctx")
    chunk = x.shape[1] // size
    return jnp.concatenate(
        [lax.dynamic_slice_in_dim(x, (ctx ^ rel_of(p)) * chunk, chunk, 1) for p in range(size)], axis=1
    )


def from_places(x):
    size, ctx = lax.axis_size("ctx"), lax.axis_index("ctx")
    chunk = x.shape[1] // size
    half = size // 2

    def place(natural):
        rel = ctx ^ natural
        return (rel % 2) * half + rel // 2

    return jnp.concatenate(
        [lax.dynamic_slice_in_dim(x, place(j) * chunk, chunk, 1) for j in range(size)], axis=1
    )


def sum_gains(terms):
    size, tp, me = lax.axis_size("ctx"), lax.axis_size("tp"), lax.axis_index("tp")
    rows, width = terms.shape
    chunk = width // size
    now = {p: terms[:, p * chunk : (p + 1) * chunk] for p in range(size)}
    now = {rel_of(p): v for p, v in now.items()}
    for bit in range(ctx_bits()):
        mask = 1 << bit
        sent = [r for r in now if r & mask]
        came = swap(jnp.concatenate([now[r] for r in sent], axis=0), bit)
        came = {r ^ mask: came[n * rows : (n + 1) * rows] for n, r in enumerate(sent)}
        now = {r: v + came[r] for r, v in now.items() if not r & mask}
    mine = now[0]
    per = rows // tp

    def rows_of(shift):
        return lax.dynamic_slice_in_dim(mine, ((me + shift) % tp) * per, per, 0)

    total = rows_of(0)
    for shift in range(1, tp):
        total = total + lax.ppermute(rows_of(shift), "tp", [(i, (i + shift) % tp) for i in range(tp)])
    return total


def on_device(
    tokens,
    cotangent,
    w_query,
    key_projection,
    value_projection,
    w_out,
    w_gate,
    w_up,
    w_down,
    norm_gains,
    block_mask,
    block_seq,
    block_place,
):
    per_device = tokens.shape[0] // BLOCK_TOKENS
    scale = HEAD_SIZE ** (-0.5)
    q_cols, kv_cols = w_query.shape[1], key_projection.shape[1]

    gain_pieces = gather_half(norm_gains, list(range(ctx_bits())))
    gains = 1.0 + jnp.concatenate(gain_pieces, axis=1).astype(F32)
    tokens = to_places(tokens)
    cot = to_places(cotangent).astype(F32)
    index, count = visible_lists(block_mask, block_seq, block_place, per_device)

    wide = gather_rows(jnp.concatenate([w_query, key_projection, value_projection], axis=1))
    rows_in = gather_tp(tokens).astype(F32)
    normed = (rows_in * inv_rms(rows_in) * gains[0]).astype(BF16)
    qkv = dot(normed, wide)
    q = (qkv[:, :q_cols] * scale).astype(BF16)
    keys_own = qkv[:, q_cols : q_cols + kv_cols].astype(BF16)
    values_own = qkv[:, q_cols + kv_cols :].astype(BF16)
    key_pieces, value_pieces = gather_ctx(keys_own, values_own)
    keys, values = jnp.concatenate(key_pieces, axis=0), jnp.concatenate(value_pieces, axis=0)

    out_t = gather_rows(w_out.T)
    gate_w = gather_rows(w_gate)
    up_w = gather_rows(w_up)
    down_t = gather_rows(w_down.T)

    outcome, totals = attend(index, count, q, keys, values)
    attended = outcome.astype(BF16)
    branch = scatter_tp(dot_back(attended, out_t).astype(BF16))

    xf = tokens.astype(F32)
    s_branch = inv_rms(branch)
    hidden = xf + branch * s_branch * gains[1]
    s_hidden = inv_rms(hidden)
    inner = gather_tp((hidden * s_hidden * gains[2]).astype(BF16))
    gate_pre = dot(inner, gate_w)
    up_pre = dot(inner, up_w)
    cube = 0.7978845608028654
    bend = jnp.tanh(cube * (gate_pre + 0.044715 * gate_pre * gate_pre * gate_pre))
    gelu = 0.5 * gate_pre * (1.0 + bend)
    mid = (gelu * up_pre).astype(BF16)
    feed = scatter_tp(dot_back(mid, down_t).astype(BF16))
    s_feed = inv_rms(feed)
    mixed = from_places((hidden + feed * s_feed * gains[3]).astype(BF16))
    term_four = jnp.sum(cot * feed * s_feed, axis=0)
    dfeed = gather_tp(norm_input_grad(feed, s_feed, gains[3], cot).astype(BF16))

    grad_down = scatter_grad(dfeed, mid).T
    dmid = dot(dfeed, down_t)
    slope = 0.5 * (1.0 + bend) + 0.5 * gate_pre * (1.0 - bend * bend) * cube * (
        1.0 + 3 * 0.044715 * gate_pre * gate_pre
    )
    dgate = (dmid * up_pre * slope).astype(BF16)
    dup = (dmid * gelu).astype(BF16)
    dinner = scatter_tp((dot_back(dgate, gate_w) + dot_back(dup, up_w)).astype(BF16))
    grad_gate = scatter_grad(inner, dgate)
    grad_up = scatter_grad(inner, dup)
    term_three = jnp.sum(dinner * hidden * s_hidden, axis=0)
    dhidden = cot + norm_input_grad(hidden, s_hidden, gains[2], dinner)
    term_two = jnp.sum(dhidden * branch * s_branch, axis=0)
    dbranch = gather_tp(norm_input_grad(branch, s_branch, gains[1], dhidden).astype(BF16))
    grad_out = scatter_grad(dbranch, attended).T
    dattended = dot(dbranch, out_t).astype(BF16)

    dq, dk, dv = attend_back(index, count, q, dattended, outcome, totals, keys, values)
    dq = dq * jnp.asarray(scale, BF16)
    size = lax.axis_size("ctx")
    group = keys_own.shape[0]
    parts = []
    for d in (dk, dv):
        parts += [d[size // 2 * group :].reshape(size // 2, group, kv_cols), d[: size // 2 * group].reshape(size // 2, group, kv_cols)]
    dkeys, dvalues = scatter_pair(*parts)
    dqkv = jnp.concatenate([dq, dkeys.astype(BF16), dvalues.astype(BF16)], axis=1)
    dnormed_part = dot_back(dqkv, wide)
    term_one = jnp.sum(dnormed_part * rows_in * inv_rms(rows_in), axis=0)
    grad_query = scatter_grad(normed, dqkv[:, :q_cols])
    grad_kv = scatter_grad(normed, dqkv[:, q_cols:])
    grad_gains = sum_gains(jnp.stack([term_one, term_two, term_three, term_four]))
    dnormed = scatter_tp(dnormed_part.astype(BF16))
    grad_tokens = from_places(dhidden + norm_input_grad(xf, inv_rms(xf), gains[0], dnormed))
    return (
        mixed,
        grad_tokens,
        grad_query,
        grad_kv[:, :kv_cols],
        grad_kv[:, kv_cols:],
        grad_out,
        grad_gate,
        grad_up,
        grad_down,
        grad_gains,
    )


def solution(mesh):
    rows, weight, turned = P(("ctx", "tp"), None), P("ctx", "tp"), P("tp", "ctx")
    in_specs = (rows, rows, weight, weight, weight, turned, weight, weight, turned, P(None, "ctx"), P(), P(), P())
    out_specs = (rows, rows, weight, weight, weight, turned, weight, weight, turned, turned)
    return jax.shard_map(on_device, mesh=mesh, in_specs=in_specs, out_specs=out_specs, check_vma=False)
```

```python
import functools
import itertools

import jax
import jax.numpy as jnp
from jax import lax
from jax.experimental import pallas as pl
from jax.experimental.pallas import tpu as pltpu
from jax.sharding import PartitionSpec as P

QUERY_HEADS = 8
KEY_VALUE_HEADS = 4
HEAD_SIZE = 256
SCORE_SOFT_LIMIT = 50
BLOCK_TOKENS = 128
EPSILON = 1e-06
KEY_STEP = 4

F32 = jnp.float32
BF16 = jnp.bfloat16


def dot(a, b):
    return jnp.dot(a, b, preferred_element_type=F32)


def dot_back(a, b):
    return lax.dot_general(a, b, (((1,), (1,)), ((), ())), preferred_element_type=F32)


def dot_rows(a, b):
    return lax.dot_general(a, b, (((0,), (0,)), ((), ())), preferred_element_type=F32)


def inv_rms(v):
    return lax.rsqrt(jnp.mean(v * v, axis=-1, keepdims=True) + EPSILON)


def norm_input_grad(v, s, gain, c):
    cw = c * gain
    return s * cw - v * (s * s * s) * jnp.mean(cw * v, axis=-1, keepdims=True)


def outer_bits(odd):
    size = lax.axis_size("ctx")
    bits = size.bit_length() - 1
    assert size == 1 << bits and bits >= 1
    order = list(range(bits - 1, 0, -1))
    return order[::-1] if odd else order


def steps_of_hops():
    return len(outer_bits(0))


def places():
    return list(itertools.product((0, 1), repeat=steps_of_hops()))


def flipped(t, s, value):
    return t[:s] + (value,) + t[s + 1 :]


def distances(odd):
    order = outer_bits(odd)
    return [c + sum(b << o for b, o in zip(t, order)) for c in (0, 1) for t in places()]


def owners():
    ctx = lax.axis_index("ctx")
    rel = jnp.where(ctx % 2 == 0, jnp.array(distances(0), jnp.int32), jnp.array(distances(1), jnp.int32))
    return ctx ^ rel


def tie(x, earlier):
    return lax.optimization_barrier((x, earlier))[0]


def tie_all(x, earlier):
    for e in earlier:
        x = tie(x, e)
    return x


def cut_rows(x, count):
    rows = x.shape[0] // count
    return [x[i * rows : (i + 1) * rows] for i in range(count)]


class Lanes:
    def __init__(self):
        self.sent = {"far": [], "near": []}
        self.depth = {"far": 2, "near": 1}

    def send(self, lane, x, pairs, after=()):
        done, depth = self.sent[lane], self.depth[lane]
        if len(done) >= depth:
            x = tie(x, done[-depth])
        x = tie_all(x, after)
        done.append(lax.ppermute(x, "ctx", pairs))
        return done[-1]

    def hop(self, x, s, after):
        orders = outer_bits(0), outer_bits(1)
        return self.send("far", x, [(i, i ^ (1 << orders[i % 2][s])) for i in range(lax.axis_size("ctx"))], after)

    def near(self, x):
        return self.send("near", x, [(i, i ^ 1) for i in range(lax.axis_size("ctx"))])


class Gather:
    def __init__(self, lanes, x):
        self.lanes, self.held, self.other = lanes, {(0,) * steps_of_hops(): x}, {}
        self.todo, self.after = self.plan(), ()

    def plan(self):
        held = self.held
        for s in range(steps_of_hops()):
            for t in list(held):
                held[flipped(t, s, 1)] = self.lanes.hop(held[t], s, self.after)
                self.after = ()
                yield

    def step(self, count=1, after=()):
        self.after = after
        for _ in range(count):
            next(self.todo, None)
        return self

    def pieces(self):
        for _ in self.todo:
            pass
        for t, v in self.held.items():
            self.other[t[::-1]] = self.lanes.near(v)
        return [half[t] for half in (self.held, self.other) for t in places()]

    def rows(self):
        return jnp.concatenate(self.pieces(), axis=0)


class Scatter:
    def __init__(self, lanes, sent, kept, after=()):
        self.lanes, self.came = lanes, []
        lanes.depth = {"far": 1, "near": 4}
        self.got = [lanes.near(tie_all(v.astype(BF16), after)) for v in sent]
        spots = places()
        back = [spots.index(t[::-1]) for t in spots]
        pairs = [(kept[i], self.got[back[i]]) for i in range(len(spots))]
        self.now = {t: k.astype(F32) + g.astype(F32) for t, (k, g) in zip(spots, pairs)}
        self.pack()

    def pack(self):
        self.gone = [t for t in self.now if t[len(self.came)]]
        self.out = jnp.concatenate([self.now[t].astype(BF16) for t in self.gone], axis=0)

    def hop(self, after=()):
        s = len(self.came)
        came = self.lanes.hop(self.out, s, after)
        self.came.append(came)
        parts = dict(zip(self.gone, cut_rows(came, len(self.gone))))
        self.now = {t: v + parts[flipped(t, s, 1)].astype(F32) for t, v in self.now.items() if not t[s]}
        if s + 1 < steps_of_hops():
            self.pack()
        return self

    def result(self):
        while len(self.came) < steps_of_hops():
            self.hop()
        (value,) = self.now.values()
        return value


def owner_at(p):
    ctx = lax.axis_index("ctx")
    return ctx ^ jnp.where(ctx % 2 == 0, distances(0)[p], distances(1)[p])


def scatter_grad(lanes, left, right, after=()):
    size = lax.axis_size("ctx")
    chunk = left.shape[1] // size
    part = dot_rows(left, right).astype(BF16)
    half = [owner_at(n) // 2 for n in range(size // 2)]
    core = lax.axis_index("ctx") % 2

    def chunks(side):
        return [lax.dynamic_slice_in_dim(part, (2 * at + side) * chunk, chunk, 0) for at in half]

    return Scatter(lanes, chunks(1 - core), chunks(core), after)


def gather_tp(x, axis=0):
    return lax.all_gather(x, "tp", axis=axis, tiled=True)


def scatter_tp(part):
    return lax.psum_scatter(part.astype(BF16), "tp", scatter_dimension=0, tiled=True).astype(F32)


def gather_line(x, axis=0, steps=None):
    size, me = lax.axis_size("tp"), lax.axis_index("tp")
    up, down = x, x
    ups, downs = {}, {}
    for s in range(1, size):
        up = lax.ppermute(up, "tp", [(i, i + 1) for i in range(s - 1, size - 1)])
        down = lax.ppermute(down, "tp", [(i, i - 1) for i in range(1, size - s + 1)])
        ups[s], downs[s] = up, down
        if steps is not None:
            steps.append([up, down])
    length = x.shape[axis]
    shape = x.shape[:axis] + (size * length,) + x.shape[axis + 1 :]
    out = lax.dynamic_update_slice_in_dim(jnp.zeros(shape, x.dtype), x, me * length, axis)
    for s in range(1, size):
        came = jnp.where(me >= s, ups[s], downs[size - s])
        out = lax.dynamic_update_slice_in_dim(out, came, (me - s + size) % size * length, axis)
    return out


def exchange_tp(take, axis):
    size, me = lax.axis_size("tp"), lax.axis_index("tp")
    came = [take(me)] + [None] * (size - 1)
    for r in sorted(range(1, size), key=lambda r: -min(r, size - r)):
        came[size - r] = lax.ppermute(take((me + r) % size), "tp", [(i, (i + r) % size) for i in range(size)])
    length = came[0].shape[axis]
    turned = jnp.concatenate(came + came[:-1], axis=axis)
    return lax.dynamic_slice_in_dim(turned, (size - me) % size * length, size * length, axis)


def take_blocks(ref, index_ref, query_block, step, blocks):
    places = [index_ref[query_block, step * KEY_STEP + j] for j in range(KEY_STEP)]
    starts = [pl.multiple_of(p * BLOCK_TOKENS, BLOCK_TOKENS) for p in places]
    return starts, jnp.concatenate([ref[pl.ds(s, BLOCK_TOKENS), :] for s in starts], axis=0)


def stack_heads(x):
    heads = x.shape[1] // HEAD_SIZE
    return jnp.concatenate([x[:, h * HEAD_SIZE : (h + 1) * HEAD_SIZE] for h in range(heads)], axis=0)


def unstack_heads(x):
    rows = BLOCK_TOKENS
    return jnp.concatenate([x[h * rows : (h + 1) * rows] for h in range(x.shape[0] // rows)], axis=1)


def attend_kernel(index_ref, count_ref, q_ref, k_ref, v_ref, out_ref, total_ref, acc_ref):
    i = pl.program_id(0)
    count = count_ref[i]
    q = stack_heads(q_ref[...])
    acc_ref[...] = jnp.zeros_like(acc_ref)
    total_ref[...] = jnp.zeros_like(total_ref)

    def body(step, carry):
        starts, keys = take_blocks(k_ref, index_ref, i, step, KEY_STEP)
        values = jnp.concatenate([v_ref[pl.ds(s, BLOCK_TOKENS), :] for s in starts], axis=0)
        scores = dot_back(q, keys)
        grown = jnp.exp(SCORE_SOFT_LIMIT * jnp.tanh(scores * (1.0 / SCORE_SOFT_LIMIT)))
        pieces = []
        for j in range(KEY_STEP):
            seen = (step * KEY_STEP + j) < count
            piece = grown[:, j * BLOCK_TOKENS : (j + 1) * BLOCK_TOKENS]
            pieces.append(jnp.where(seen, piece, 0.0))
        total_ref[...] += functools.reduce(jnp.add, pieces)
        acc_ref[...] += dot(jnp.concatenate(pieces, axis=1).astype(BF16), values)
        return carry

    lax.fori_loop(0, (count + KEY_STEP - 1) // KEY_STEP, body, 0)
    totals = jnp.sum(total_ref[...], axis=1, keepdims=True)
    total_ref[...] = jnp.broadcast_to(totals, total_ref.shape)
    out_ref[...] = unstack_heads(acc_ref[...] / totals)


def attend_back_kernel(
    index_ref, count_ref, q_ref, dout_ref, out_ref, total_ref, k_ref, v_ref, dq_ref, dkv_ref, acc_ref
):
    i = pl.program_id(0)

    @pl.when(i == 0)
    def _():
        dkv_ref[...] = jnp.zeros_like(dkv_ref)

    count = count_ref[i]
    q = stack_heads(q_ref[...])
    dout = stack_heads(dout_ref[...]).astype(F32)
    inverse = 1.0 / total_ref[:, :1]
    scaled = (dout * inverse).astype(BF16)
    weighted = dout * stack_heads(out_ref[...]) * inverse
    ones = jnp.ones((8, HEAD_SIZE), F32)
    dtotal = -lax.dot_general(
        ones, weighted, (((1,), (1,)), ((), ())), precision=lax.Precision.HIGHEST, preferred_element_type=F32
    )[:1]
    acc_ref[...] = jnp.zeros_like(acc_ref)

    def body(step, carry):
        starts, keys = take_blocks(k_ref, index_ref, i, step, KEY_STEP)
        values = jnp.concatenate([v_ref[pl.ds(s, BLOCK_TOKENS), :] for s in starts], axis=0)
        soft = jnp.tanh(dot_back(keys, q) * (1.0 / SCORE_SOFT_LIMIT))
        grown = jnp.exp(SCORE_SOFT_LIMIT * soft)
        pieces = []
        for j in range(KEY_STEP):
            seen = (step * KEY_STEP + j) < count
            piece = grown[j * BLOCK_TOKENS : (j + 1) * BLOCK_TOKENS]
            pieces.append(jnp.where(seen, piece, 0.0))
        grown = jnp.concatenate(pieces, axis=0)
        dprob = dot_back(values, scaled)
        dscores = (grown * (dprob + dtotal) * (1.0 - soft * soft)).astype(BF16)
        acc_ref[...] += dot_rows(dscores, keys)
        dkeys = dot(dscores, q)
        dvalues = dot(grown.astype(BF16), scaled)
        for j in range(KEY_STEP):
            at = pl.ds(starts[j], BLOCK_TOKENS)
            dkv_ref[at, :HEAD_SIZE] += dkeys[j * BLOCK_TOKENS : (j + 1) * BLOCK_TOKENS]
            dkv_ref[at, HEAD_SIZE:] += dvalues[j * BLOCK_TOKENS : (j + 1) * BLOCK_TOKENS]
        return carry

    lax.fori_loop(0, (count + KEY_STEP - 1) // KEY_STEP, body, 0)
    dq_ref[...] = unstack_heads(acc_ref[...]).astype(BF16)


VMEM_LIMIT = 56 * 1024 * 1024


def whole_spec(rows, columns, at=0):
    return pl.BlockSpec((rows, columns), lambda i, *_: (0, at), pipeline_mode=pl.Buffered(1))


def row_spec(rows, columns):
    return pl.BlockSpec((rows, columns), lambda i, *_: (i, 0))


def attend(index, count, q, kv):
    rows, columns = q.shape
    blocks, stacked = rows // BLOCK_TOKENS, BLOCK_TOKENS * (columns // HEAD_SIZE)
    return pl.pallas_call(
        attend_kernel,
        grid_spec=pltpu.PrefetchScalarGridSpec(
            num_scalar_prefetch=2,
            grid=(blocks,),
            in_specs=[row_spec(BLOCK_TOKENS, columns), whole_spec(kv.shape[0], HEAD_SIZE), whole_spec(kv.shape[0], HEAD_SIZE, 1)],
            out_specs=[row_spec(BLOCK_TOKENS, columns), row_spec(stacked, BLOCK_TOKENS)],
            scratch_shapes=[pltpu.VMEM((stacked, HEAD_SIZE), F32)],
        ),
        out_shape=[
            jax.ShapeDtypeStruct((rows, columns), F32),
            jax.ShapeDtypeStruct((blocks * stacked, BLOCK_TOKENS), F32),
        ],
        compiler_params=pltpu.CompilerParams(vmem_limit_bytes=VMEM_LIMIT),
        cost_estimate=pl.CostEstimate(flops=2 * rows * columns * kv.shape[0], bytes_accessed=6 << 20, transcendentals=0),
    )(index, count, q, kv, kv)


def attend_back(index, count, q, dout, out, totals, kv):
    rows, columns = q.shape
    blocks, stacked = rows // BLOCK_TOKENS, BLOCK_TOKENS * (columns // HEAD_SIZE)
    row = row_spec(BLOCK_TOKENS, columns)
    return pl.pallas_call(
        attend_back_kernel,
        grid_spec=pltpu.PrefetchScalarGridSpec(
            num_scalar_prefetch=2,
            grid=(blocks,),
            in_specs=[row, row, row, row_spec(stacked, BLOCK_TOKENS)]
            + [whole_spec(kv.shape[0], HEAD_SIZE), whole_spec(kv.shape[0], HEAD_SIZE, 1)],
            out_specs=[row, whole_spec(*kv.shape)],
            scratch_shapes=[pltpu.VMEM((stacked, HEAD_SIZE), F32)],
        ),
        out_shape=[
            jax.ShapeDtypeStruct((rows, columns), BF16),
            jax.ShapeDtypeStruct(kv.shape, F32),
        ],
        compiler_params=pltpu.CompilerParams(vmem_limit_bytes=VMEM_LIMIT),
        cost_estimate=pl.CostEstimate(flops=5 * rows * columns * kv.shape[0], bytes_accessed=16 << 20, transcendentals=0),
    )(index, count, q, dout, out, totals, kv, kv)


GELU = 0.7978845608028654
CUBIC = 0.044715
TILE = 256


def ffn_in_kernel(x_ref, gate_w_ref, up_w_ref, gate_ref, up_ref, mid_ref):
    x = x_ref[...]
    gate_pre = dot(x, gate_w_ref[...])
    up_pre = dot(x, up_w_ref[...])
    bend = jnp.tanh(GELU * (gate_pre + CUBIC * gate_pre * gate_pre * gate_pre))
    gate_ref[...] = gate_pre
    up_ref[...] = up_pre
    mid_ref[...] = (0.5 * gate_pre * (1.0 + bend) * up_pre).astype(BF16)


def ffn_in(x, pair_w):
    rows, depth = x.shape
    columns = pair_w.shape[1] // 2
    steps = columns // TILE
    tile = pl.BlockSpec((rows, TILE), lambda i: (0, i))
    return pl.pallas_call(
        ffn_in_kernel,
        grid=(steps,),
        in_specs=[
            pl.BlockSpec((rows, depth), lambda i: (0, 0), pipeline_mode=pl.Buffered(1)),
            pl.BlockSpec((depth, TILE), lambda i: (0, i)),
            pl.BlockSpec((depth, TILE), lambda i: (0, i + steps)),
        ],
        out_specs=[tile] * 3,
        out_shape=[jax.ShapeDtypeStruct((rows, columns), t) for t in (F32, F32, BF16)],
        compiler_params=pltpu.CompilerParams(vmem_limit_bytes=VMEM_LIMIT),
        cost_estimate=pl.CostEstimate(flops=4 * rows * depth * columns, bytes_accessed=4 * depth * columns, transcendentals=0),
        name="ffn_in",
    )(x, pair_w, pair_w)


def ffn_back_kernel(x_ref, gate_ref, up_ref, w_ref, dgate_ref, dup_ref):
    dmid = dot(x_ref[...], w_ref[...])
    gate_pre, up_pre = gate_ref[...], up_ref[...]
    square = gate_pre * gate_pre
    bend = jnp.tanh(GELU * (gate_pre + CUBIC * square * gate_pre))
    slope = 0.5 * (1.0 + bend) + 0.5 * gate_pre * (1.0 - bend * bend) * GELU * (1.0 + 3 * CUBIC * square)
    dgate_ref[...] = (dmid * up_pre * slope).astype(BF16)
    dup_ref[...] = (dmid * (0.5 * gate_pre * (1.0 + bend))).astype(BF16)


def ffn_back(x, gate_pre, up_pre, down_t):
    rows, depth = x.shape
    columns = down_t.shape[1]
    tile = pl.BlockSpec((rows, TILE), lambda i: (0, i))
    return pl.pallas_call(
        ffn_back_kernel,
        grid=(columns // TILE,),
        in_specs=[
            pl.BlockSpec((rows, depth), lambda i: (0, 0), pipeline_mode=pl.Buffered(1)),
            tile,
            tile,
            pl.BlockSpec((depth, TILE), lambda i: (0, i)),
        ],
        out_specs=[tile] * 2,
        out_shape=[jax.ShapeDtypeStruct((rows, columns), BF16)] * 2,
        compiler_params=pltpu.CompilerParams(vmem_limit_bytes=VMEM_LIMIT),
        cost_estimate=pl.CostEstimate(flops=2 * rows * depth * columns, bytes_accessed=2 * depth * columns, transcendentals=0),
        name="ffn_back",
    )(x, gate_pre, up_pre, down_t)


def rows_kernel(terms, *refs):
    xs, w_ref, out_ref = refs[:terms], refs[terms], refs[terms + 1]
    depth = xs[0].shape[1]
    total = 0.0
    for m in range(terms):
        total = total + dot_back(xs[m][...], w_ref[:, m * depth : (m + 1) * depth])
    out_ref[...] = total.astype(BF16)


def rows_call(xs, w, name):
    rows, depth = xs[0].shape
    width, terms = w.shape[0], len(xs)
    return pl.pallas_call(
        functools.partial(rows_kernel, terms),
        grid=(width // TILE,),
        in_specs=[pl.BlockSpec((rows, depth), lambda i: (0, 0), pipeline_mode=pl.Buffered(1))] * terms
        + [pl.BlockSpec((TILE, terms * depth), lambda i: (i, 0))],
        out_specs=pl.BlockSpec((rows, TILE), lambda i: (0, i)),
        out_shape=jax.ShapeDtypeStruct((rows, width), BF16),
        compiler_params=pltpu.CompilerParams(vmem_limit_bytes=VMEM_LIMIT),
        cost_estimate=pl.CostEstimate(
            flops=2 * rows * depth * width * terms, bytes_accessed=2 * depth * width * terms, transcendentals=0
        ),
        name=name,
    )(*xs, w)


def visible_lists(block_mask, block_seq, block_place, per_device):
    tp = lax.axis_size("tp")
    ctx = lax.axis_index("ctx")
    total = block_seq.shape[0]
    owner = owners()
    of_group = tp * per_device
    inner = jnp.arange(of_group, dtype=jnp.int32)
    query_ids = ctx * of_group + inner
    key_ids = (owner[:, None] * of_group + inner[None, :]).reshape(-1)
    every = jnp.arange(total, dtype=jnp.int32)

    def look_up(ids, table):
        return jnp.sum(jnp.where(ids[:, None] == every[None, :], table[None, :], 0), axis=1)

    places = jnp.arange(block_mask.shape[0], dtype=jnp.int32)
    query_pick = (look_up(query_ids, block_place)[:, None] == places[None, :]).astype(F32)
    key_pick = (look_up(key_ids, block_place)[:, None] == places[None, :]).astype(F32)
    hits = dot_back(dot(query_pick, block_mask.astype(F32)), key_pick)
    same = look_up(query_ids, block_seq)[:, None] == look_up(key_ids, block_seq)[None, :]
    seen = (hits > 0.5) & same
    before = (every[:, None] < every[None, :]).astype(F32)
    rank = dot(seen.astype(F32), before).astype(jnp.int32)
    wanted = seen[:, None, :] & (rank[:, None, :] == every[None, :, None])
    index = jnp.sum(jnp.where(wanted, every[None, None, :], 0), axis=2)
    index = jnp.pad(index, ((0, 0), (0, KEY_STEP)))
    return index, jnp.sum(seen.astype(jnp.int32), axis=1)


def gather_small(x):
    size = lax.axis_size("ctx")
    orders = outer_bits(0), outer_bits(1)
    held = {(0,) * steps_of_hops(): x}
    rows = x.shape[0]

    def send(pairs):
        came = lax.ppermute(jnp.concatenate(list(held.values()), axis=0), "ctx", pairs)
        return {t: came[n * rows : (n + 1) * rows] for n, t in enumerate(held)}

    for s in range(steps_of_hops()):
        came = send([(i, i ^ (1 << orders[i % 2][s])) for i in range(size)])
        held |= {flipped(t, s, 1): v for t, v in came.items()}
    other = {t[::-1]: v for t, v in send([(i, i ^ 1) for i in range(size)]).items()}
    blocks = jnp.stack([half[t] for half in (held, other) for t in places()])
    spots = []
    for j in range(size):
        found = [jnp.where(owner_at(p) == j, p, 0) for p in range(size)]
        spots.append(functools.reduce(jnp.add, found))
    return jnp.concatenate([lax.dynamic_index_in_dim(blocks, at, 0, keepdims=False) for at in spots], axis=1)


def sum_gains(terms):
    size, tp, me = lax.axis_size("ctx"), lax.axis_size("tp"), lax.axis_index("tp")
    orders = outer_bits(0), outer_bits(1)
    rows, width = terms.shape
    chunk, half = width // size, size // 2
    spots = places()
    parts = [lax.dynamic_slice_in_dim(terms, owner_at(p) * chunk, chunk, 1) for p in range(size)]

    def send(values, pairs):
        came = lax.ppermute(jnp.concatenate(values, axis=0), "ctx", pairs)
        return [came[n * rows : (n + 1) * rows] for n in range(len(values))]

    came = send(parts[half:], [(i, i ^ 1) for i in range(size)])
    now = {t: parts[n] + came[spots.index(t[::-1])] for n, t in enumerate(spots)}
    for s in range(steps_of_hops()):
        gone = [t for t in now if t[s]]
        came = send([now[t] for t in gone], [(i, i ^ (1 << orders[i % 2][s])) for i in range(size)])
        came = {flipped(t, s, 0): v for t, v in zip(gone, came)}
        now = {t: v + came[t] for t, v in now.items() if not t[s]}
    (mine,) = now.values()
    per = rows // tp

    def rows_of(shift):
        return lax.dynamic_slice_in_dim(mine, ((me + shift) % tp) * per, per, 0)

    total = rows_of(0)
    for shift in range(1, tp):
        total = total + lax.ppermute(rows_of(shift), "tp", [(i, (i + shift) % tp) for i in range(tp)])
    return total


def on_device(
    tokens,
    cotangent,
    w_query,
    key_projection,
    value_projection,
    w_out,
    w_gate,
    w_up,
    w_down,
    norm_gains,
    block_mask,
    block_seq,
    block_place,
):
    per_device = tokens.shape[0] // BLOCK_TOKENS
    scale = HEAD_SIZE ** (-0.5)
    q_cols, kv_cols = w_query.shape[1], key_projection.shape[1]
    in_cols = q_cols + 2 * kv_cols
    lanes = Lanes()

    def gather_weight(w):
        return lax.all_gather(w, "ctx", axis=0, tiled=True)

    wide = gather_weight(jnp.concatenate([w_query, key_projection, value_projection, w_out.T], axis=1))
    gains = 1.0 + gather_small(norm_gains).astype(F32)
    cot = cotangent.astype(F32)
    index, count = visible_lists(block_mask, block_seq, block_place, per_device)

    rows_in = gather_line(tokens)
    pair_w = gather_weight(tie_all(jnp.concatenate([w_gate, w_up], axis=1), [wide, rows_in]))
    half = wide.shape[0] // 2
    core = lax.axis_index("ctx") % 2
    out_half = lax.dynamic_slice_in_dim(wide, core * half, half, 0)[:, in_cols:]
    out_steps, inner_steps = [], []
    out_half = gather_line(tie(out_half, rows_in), axis=1, steps=out_steps)
    wide = wide[:, :in_cols]
    rows_in = rows_in.astype(F32)
    normed = (rows_in * inv_rms(rows_in) * gains[0]).astype(BF16)
    qkv = dot(normed, wide)
    q = (qkv[:, :q_cols] * scale).astype(BF16)
    kv_own = qkv[:, q_cols:].astype(BF16)
    kv = tie_all(Gather(lanes, kv_own).rows(), out_steps[0])

    outcome, totals = attend(index, count, q, kv)
    attended = tie_all(outcome.astype(BF16), out_steps[1])
    rows = tokens.shape[0]
    own_heads = exchange_tp(lambda i: lax.dynamic_slice_in_dim(attended, i * rows, rows, 0), 1)
    out_other = lanes.near(tie(out_half, attended))
    out_t = jnp.zeros((2 * half, out_half.shape[1]), BF16)
    out_t = lax.dynamic_update_slice_in_dim(out_t, out_half, core * half, 0)
    out_t = lax.dynamic_update_slice_in_dim(out_t, out_other, (1 - core) * half, 0)
    branch = dot_back(own_heads, out_t)
    size = lax.axis_size("ctx")

    xf = tokens.astype(F32)
    s_branch = inv_rms(branch)
    hidden = xf + branch * s_branch * gains[1]
    s_hidden = inv_rms(hidden)
    inner = gather_line((hidden * s_hidden * gains[2]).astype(BF16), steps=inner_steps)
    down_t = gather_weight(tie_all(w_down.T, [pair_w] + inner_steps[0]))
    gate_pre, up_pre, mid = ffn_in(inner, pair_w)
    feed = scatter_tp(rows_call([mid], down_t, "ffn_out"))
    s_feed = inv_rms(feed)
    mixed = (hidden + feed * s_feed * gains[3]).astype(BF16)
    term_four = jnp.sum(cot * feed * s_feed, axis=0)
    dfeed = gather_tp(norm_input_grad(feed, s_feed, gains[3], cot).astype(BF16))

    down = scatter_grad(lanes, dfeed, mid)
    dgate, dup = ffn_back(dfeed, gate_pre, up_pre, down_t)
    dinner_part = rows_call([tie(dgate, down.out), dup], pair_w, "ffn_back_in")
    down.hop()
    gate = scatter_grad(lanes, inner, tie(dgate, dinner_part), [down.came[0]])
    down.hop()
    gate.hop()
    dinner = tie_all(scatter_tp(dinner_part), [down.came[1], gate.out])
    down_sum = down.result()
    term_three = jnp.sum(dinner * hidden * s_hidden, axis=0)
    dhidden = cot + norm_input_grad(hidden, s_hidden, gains[2], dinner)
    term_two = jnp.sum(dhidden * branch * s_branch, axis=0)
    dbranch = norm_input_grad(branch, s_branch, gains[1], dhidden).astype(BF16)
    dheads = dot(dbranch, out_t).astype(BF16)
    head_cols = attended.shape[1]
    dattended = exchange_tp(lambda i: lax.dynamic_slice_in_dim(dheads, i * head_cols, head_cols, 1), 0)
    dattended = tie_all(dattended, [gate.came[0]])
    up = scatter_grad(lanes, inner, tie(dup, dheads))
    gate.hop([dheads])
    dbranch = gather_tp(dbranch)

    dq, dkv = attend_back(index, count, q, dattended, outcome, totals, kv)
    dq = dq * jnp.asarray(scale, BF16)
    dkv = tie_all(dkv, [gate.came[1]] + up.got)
    dkv = dkv.reshape(2, size // 2, kv_own.shape[0], 2 * kv_cols)
    dkv_own = Scatter(lanes, dkv[1], dkv[0]).result().astype(BF16)
    up.hop()
    grad_up = up.result()
    grad_gate = gate.result()
    dqkv = jnp.concatenate([dq, dkv_own], axis=1)
    dnormed_part = dot_back(dqkv, wide).astype(BF16)
    grad_out = scatter_grad(lanes, tie(dbranch, dnormed_part), attended).result()
    grad_query = scatter_grad(lanes, normed, tie(dq, dnormed_part)).result()
    term_one = jnp.sum(dnormed_part.astype(F32) * rows_in * inv_rms(rows_in), axis=0)
    grad_kv = scatter_grad(lanes, normed, tie(dkv_own, dnormed_part)).result()
    dnormed = tie_all(scatter_tp(dnormed_part), [grad_up, grad_out])
    grad_gains = sum_gains(jnp.stack([term_one, term_two, term_three, term_four]))
    grad_tokens = dhidden + norm_input_grad(xf, inv_rms(xf), gains[0], dnormed)
    return (
        mixed,
        grad_tokens,
        grad_query,
        grad_kv[:, :kv_cols],
        grad_kv[:, kv_cols:],
        grad_out.T,
        grad_gate,
        grad_up,
        down_sum.T,
        grad_gains,
    )


def solution(mesh):
    rows, weight, turned = P(("ctx", "tp"), None), P("ctx", "tp"), P("tp", "ctx")
    in_specs = (rows, rows, weight, weight, weight, turned, weight, weight, turned, P(None, "ctx"), P(), P(), P())
    out_specs = (rows, rows, weight, weight, weight, turned, weight, weight, turned, turned)
    return jax.shard_map(on_device, mesh=mesh, in_specs=in_specs, out_specs=out_specs, check_vma=False)
```

```python
import functools
import itertools

import jax
import jax.numpy as jnp
from jax import lax
from jax.experimental import pallas as pl
from jax.experimental.pallas import tpu as pltpu
from jax.sharding import PartitionSpec as P

QUERY_HEADS = 8
KEY_VALUE_HEADS = 4
HEAD_SIZE = 256
SCORE_SOFT_LIMIT = 50
BLOCK_TOKENS = 128
EPSILON = 1e-06
KEY_STEP = 4

F32 = jnp.float32
BF16 = jnp.bfloat16


def dot(a, b):
    return jnp.dot(a, b, preferred_element_type=F32)


def dot_back(a, b):
    return lax.dot_general(a, b, (((1,), (1,)), ((), ())), preferred_element_type=F32)


def dot_rows(a, b):
    return lax.dot_general(a, b, (((0,), (0,)), ((), ())), preferred_element_type=F32)


def inv_rms(v):
    return lax.rsqrt(jnp.mean(v * v, axis=-1, keepdims=True) + EPSILON)


def norm_input_grad(v, s, gain, c):
    cw = c * gain
    return s * cw - v * (s * s * s) * jnp.mean(cw * v, axis=-1, keepdims=True)


def outer_bits(odd):
    size = lax.axis_size("ctx")
    bits = size.bit_length() - 1
    assert size == 1 << bits and bits >= 1
    order = list(range(bits - 1, 0, -1))
    return order[::-1] if odd else order


def steps_of_hops():
    return len(outer_bits(0))


def places():
    return list(itertools.product((0, 1), repeat=steps_of_hops()))


def flipped(t, s, value):
    return t[:s] + (value,) + t[s + 1 :]


def distances(odd):
    order = outer_bits(odd)
    return [c + sum(b << o for b, o in zip(t, order)) for c in (0, 1) for t in places()]


def owners():
    ctx = lax.axis_index("ctx")
    rel = jnp.where(ctx % 2 == 0, jnp.array(distances(0), jnp.int32), jnp.array(distances(1), jnp.int32))
    return ctx ^ rel


def tie(x, earlier):
    return lax.optimization_barrier((x, earlier))[0]


def tie_all(x, earlier):
    for e in earlier:
        x = tie(x, e)
    return x


def cut_rows(x, count):
    rows = x.shape[0] // count
    return [x[i * rows : (i + 1) * rows] for i in range(count)]


class Lanes:
    def __init__(self):
        self.sent = {"far": [], "near": []}
        self.depth = {"far": 2, "near": 1}

    def send(self, lane, x, pairs, after=()):
        done, depth = self.sent[lane], self.depth[lane]
        if len(done) >= depth:
            x = tie(x, done[-depth])
        x = tie_all(x, after)
        done.append(lax.ppermute(x, "ctx", pairs))
        return done[-1]

    def hop(self, x, s, after):
        orders = outer_bits(0), outer_bits(1)
        return self.send("far", x, [(i, i ^ (1 << orders[i % 2][s])) for i in range(lax.axis_size("ctx"))], after)

    def near(self, x):
        return self.send("near", x, [(i, i ^ 1) for i in range(lax.axis_size("ctx"))])


class Gather:
    def __init__(self, lanes, x):
        self.lanes, self.held, self.other = lanes, {(0,) * steps_of_hops(): x}, {}
        self.todo, self.after = self.plan(), ()

    def plan(self):
        held = self.held
        for s in range(steps_of_hops()):
            for t in list(held):
                held[flipped(t, s, 1)] = self.lanes.hop(held[t], s, self.after)
                self.after = ()
                yield

    def step(self, count=1, after=()):
        self.after = after
        for _ in range(count):
            next(self.todo, None)
        return self

    def pieces(self):
        for _ in self.todo:
            pass
        for t, v in self.held.items():
            self.other[t[::-1]] = self.lanes.near(v)
        return [half[t] for half in (self.held, self.other) for t in places()]

    def rows(self):
        return jnp.concatenate(self.pieces(), axis=0)


class Scatter:
    def __init__(self, lanes, sent, kept, after=()):
        self.lanes, self.came = lanes, []
        self.sent = sent
        lanes.depth = {"far": 1, "near": 4}
        self.got = [lanes.near(tie_all(v.astype(BF16), after)) for v in sent]
        spots = places()
        back = [spots.index(t[::-1]) for t in spots]
        pairs = [(kept[i], self.got[back[i]]) for i in range(len(spots))]
        self.now = {t: k.astype(F32) + g.astype(F32) for t, (k, g) in zip(spots, pairs)}
        self.pack()

    def pack(self):
        self.gone = [t for t in self.now if t[len(self.came)]]
        self.out = jnp.concatenate([self.now[t].astype(BF16) for t in self.gone], axis=0)

    def hop(self, after=()):
        s = len(self.came)
        came = self.lanes.hop(self.out, s, after)
        self.came.append(came)
        parts = dict(zip(self.gone, cut_rows(came, len(self.gone))))
        self.now = {t: v + parts[flipped(t, s, 1)].astype(F32) for t, v in self.now.items() if not t[s]}
        if s + 1 < steps_of_hops():
            self.pack()
        return self

    def result(self):
        while len(self.came) < steps_of_hops():
            self.hop()
        (value,) = self.now.values()
        return value


def owner_at(p):
    ctx = lax.axis_index("ctx")
    return ctx ^ jnp.where(ctx % 2 == 0, distances(0)[p], distances(1)[p])


def scatter_grads(lanes, pairs, after=()):
    size = lax.axis_size("ctx")
    parts = [dot_rows(left, right).astype(BF16) for left, right in pairs]
    chunk = parts[0].shape[0] // size
    half = [owner_at(n) // 2 for n in range(size // 2)]
    core = lax.axis_index("ctx") % 2

    def chunks(side):
        found = []
        for at in half:
            cut = [lax.dynamic_slice_in_dim(part, (2 * at + side) * chunk, chunk, 0) for part in parts]
            found.append(cut[0] if len(cut) == 1 else jnp.concatenate(cut, axis=1))
        return found

    return Scatter(lanes, chunks(1 - core), chunks(core), after)


def scatter_grad(lanes, left, right, after=()):
    return scatter_grads(lanes, [(left, right)], after)


def gather_tp(x, axis=0):
    return lax.all_gather(x, "tp", axis=axis, tiled=True)


def scatter_tp(part):
    return lax.psum_scatter(part.astype(BF16), "tp", scatter_dimension=0, tiled=True).astype(F32)


def gather_line(x, axis=0, steps=None, after={}):
    size, me = lax.axis_size("tp"), lax.axis_index("tp")
    up, down = x, x
    ups, downs = {}, {}
    for s in range(1, size):
        up, down = [tie_all(v, after.get(s, ())) for v in (up, down)]
        up = lax.ppermute(up, "tp", [(i, i + 1) for i in range(s - 1, size - 1)])
        down = lax.ppermute(down, "tp", [(i, i - 1) for i in range(1, size - s + 1)])
        ups[s], downs[s] = up, down
        if steps is not None:
            steps.append([up, down])
    length = x.shape[axis]
    shape = x.shape[:axis] + (size * length,) + x.shape[axis + 1 :]
    out = lax.dynamic_update_slice_in_dim(jnp.zeros(shape, x.dtype), x, me * length, axis)
    for s in range(1, size):
        came = jnp.where(me >= s, ups[s], downs[size - s])
        out = lax.dynamic_update_slice_in_dim(out, came, (me - s + size) % size * length, axis)
    return out


def exchange_tp(take, axis):
    size, me = lax.axis_size("tp"), lax.axis_index("tp")
    came = [take(me)] + [None] * (size - 1)
    for r in sorted(range(1, size), key=lambda r: -min(r, size - r)):
        came[size - r] = lax.ppermute(take((me + r) % size), "tp", [(i, (i + r) % size) for i in range(size)])
    length = came[0].shape[axis]
    turned = jnp.concatenate(came + came[:-1], axis=axis)
    return lax.dynamic_slice_in_dim(turned, (size - me) % size * length, size * length, axis)


def take_blocks(ref, index_ref, query_block, step, blocks):
    places = [index_ref[query_block, step * KEY_STEP + j] for j in range(KEY_STEP)]
    starts = [pl.multiple_of(p * BLOCK_TOKENS, BLOCK_TOKENS) for p in places]
    return starts, jnp.concatenate([ref[pl.ds(s, BLOCK_TOKENS), :] for s in starts], axis=0)


def stack_heads(x):
    heads = x.shape[1] // HEAD_SIZE
    return jnp.concatenate([x[:, h * HEAD_SIZE : (h + 1) * HEAD_SIZE] for h in range(heads)], axis=0)


def unstack_heads(x):
    rows = BLOCK_TOKENS
    return jnp.concatenate([x[h * rows : (h + 1) * rows] for h in range(x.shape[0] // rows)], axis=1)


def attend_kernel(index_ref, count_ref, q_ref, k_ref, v_ref, out_ref, total_ref, acc_ref):
    i = pl.program_id(0)
    count = count_ref[i]
    q = stack_heads(q_ref[...])
    acc_ref[...] = jnp.zeros_like(acc_ref)
    total_ref[...] = jnp.zeros_like(total_ref)

    def body(step, carry):
        starts, keys = take_blocks(k_ref, index_ref, i, step, KEY_STEP)
        values = jnp.concatenate([v_ref[pl.ds(s, BLOCK_TOKENS), :] for s in starts], axis=0)
        scores = dot_back(q, keys)
        grown = jnp.exp(SCORE_SOFT_LIMIT * jnp.tanh(scores * (1.0 / SCORE_SOFT_LIMIT)))
        pieces = []
        for j in range(KEY_STEP):
            seen = (step * KEY_STEP + j) < count
            piece = grown[:, j * BLOCK_TOKENS : (j + 1) * BLOCK_TOKENS]
            pieces.append(jnp.where(seen, piece, 0.0))
        total_ref[...] += functools.reduce(jnp.add, pieces)
        acc_ref[...] += dot(jnp.concatenate(pieces, axis=1).astype(BF16), values)
        return carry

    lax.fori_loop(0, (count + KEY_STEP - 1) // KEY_STEP, body, 0)
    totals = jnp.sum(total_ref[...], axis=1, keepdims=True)
    total_ref[...] = jnp.broadcast_to(totals, total_ref.shape)
    out_ref[...] = unstack_heads(acc_ref[...] / totals)


def attend_back_kernel(
    index_ref, count_ref, q_ref, dout_ref, out_ref, total_ref, k_ref, v_ref, dq_ref, dkv_ref, acc_ref
):
    i = pl.program_id(0)

    @pl.when(i == 0)
    def _():
        dkv_ref[...] = jnp.zeros_like(dkv_ref)

    count = count_ref[i]
    q = stack_heads(q_ref[...])
    dout = stack_heads(dout_ref[...]).astype(F32)
    inverse = 1.0 / total_ref[:, :1]
    scaled = (dout * inverse).astype(BF16)
    weighted = dout * stack_heads(out_ref[...]) * inverse
    ones = jnp.ones((8, HEAD_SIZE), F32)
    dtotal = -lax.dot_general(
        ones, weighted, (((1,), (1,)), ((), ())), precision=lax.Precision.HIGHEST, preferred_element_type=F32
    )[:1]
    acc_ref[...] = jnp.zeros_like(acc_ref)

    def body(step, carry):
        starts, keys = take_blocks(k_ref, index_ref, i, step, KEY_STEP)
        values = jnp.concatenate([v_ref[pl.ds(s, BLOCK_TOKENS), :] for s in starts], axis=0)
        soft = jnp.tanh(dot_back(keys, q) * (1.0 / SCORE_SOFT_LIMIT))
        grown = jnp.exp(SCORE_SOFT_LIMIT * soft)
        pieces = []
        for j in range(KEY_STEP):
            seen = (step * KEY_STEP + j) < count
            piece = grown[j * BLOCK_TOKENS : (j + 1) * BLOCK_TOKENS]
            pieces.append(jnp.where(seen, piece, 0.0))
        grown = jnp.concatenate(pieces, axis=0)
        dprob = dot_back(values, scaled)
        dscores = (grown * (dprob + dtotal) * (1.0 - soft * soft)).astype(BF16)
        acc_ref[...] += dot_rows(dscores, keys)
        dkeys = dot(dscores, q)
        dvalues = dot(grown.astype(BF16), scaled)
        for j in range(KEY_STEP):
            at = pl.ds(starts[j], BLOCK_TOKENS)
            dkv_ref[at, :HEAD_SIZE] += dkeys[j * BLOCK_TOKENS : (j + 1) * BLOCK_TOKENS]
            dkv_ref[at, HEAD_SIZE:] += dvalues[j * BLOCK_TOKENS : (j + 1) * BLOCK_TOKENS]
        return carry

    lax.fori_loop(0, (count + KEY_STEP - 1) // KEY_STEP, body, 0)
    dq_ref[...] = unstack_heads(acc_ref[...]).astype(BF16)


VMEM_LIMIT = 56 * 1024 * 1024


def whole_spec(rows, columns, at=0):
    return pl.BlockSpec((rows, columns), lambda i, *_: (0, at), pipeline_mode=pl.Buffered(1))


def row_spec(rows, columns):
    return pl.BlockSpec((rows, columns), lambda i, *_: (i, 0))


def attend(index, count, q, kv):
    rows, columns = q.shape
    blocks, stacked = rows // BLOCK_TOKENS, BLOCK_TOKENS * (columns // HEAD_SIZE)
    return pl.pallas_call(
        attend_kernel,
        grid_spec=pltpu.PrefetchScalarGridSpec(
            num_scalar_prefetch=2,
            grid=(blocks,),
            in_specs=[row_spec(BLOCK_TOKENS, columns), whole_spec(kv.shape[0], HEAD_SIZE), whole_spec(kv.shape[0], HEAD_SIZE, 1)],
            out_specs=[row_spec(BLOCK_TOKENS, columns), row_spec(stacked, BLOCK_TOKENS)],
            scratch_shapes=[pltpu.VMEM((stacked, HEAD_SIZE), F32)],
        ),
        out_shape=[
            jax.ShapeDtypeStruct((rows, columns), F32),
            jax.ShapeDtypeStruct((blocks * stacked, BLOCK_TOKENS), F32),
        ],
        compiler_params=pltpu.CompilerParams(vmem_limit_bytes=VMEM_LIMIT),
        cost_estimate=pl.CostEstimate(flops=2 * rows * columns * kv.shape[0], bytes_accessed=6 << 20, transcendentals=0),
    )(index, count, q, kv, kv)


def attend_back(index, count, q, dout, out, totals, kv):
    rows, columns = q.shape
    blocks, stacked = rows // BLOCK_TOKENS, BLOCK_TOKENS * (columns // HEAD_SIZE)
    row = row_spec(BLOCK_TOKENS, columns)
    return pl.pallas_call(
        attend_back_kernel,
        grid_spec=pltpu.PrefetchScalarGridSpec(
            num_scalar_prefetch=2,
            grid=(blocks,),
            in_specs=[row, row, row, row_spec(stacked, BLOCK_TOKENS)]
            + [whole_spec(kv.shape[0], HEAD_SIZE), whole_spec(kv.shape[0], HEAD_SIZE, 1)],
            out_specs=[row, whole_spec(*kv.shape)],
            scratch_shapes=[pltpu.VMEM((stacked, HEAD_SIZE), F32)],
        ),
        out_shape=[
            jax.ShapeDtypeStruct((rows, columns), BF16),
            jax.ShapeDtypeStruct(kv.shape, F32),
        ],
        compiler_params=pltpu.CompilerParams(vmem_limit_bytes=VMEM_LIMIT),
        cost_estimate=pl.CostEstimate(flops=5 * rows * columns * kv.shape[0], bytes_accessed=16 << 20, transcendentals=0),
    )(index, count, q, dout, out, totals, kv, kv)


GELU = 0.7978845608028654
CUBIC = 0.044715
TILE = 256


def ffn_in_kernel(x_ref, gate_w_ref, up_w_ref, gate_ref, up_ref, mid_ref):
    x = x_ref[...]
    gate_pre = dot(x, gate_w_ref[...])
    up_pre = dot(x, up_w_ref[...])
    bend = jnp.tanh(GELU * (gate_pre + CUBIC * gate_pre * gate_pre * gate_pre))
    gate_ref[...] = gate_pre
    up_ref[...] = up_pre
    mid_ref[...] = (0.5 * gate_pre * (1.0 + bend) * up_pre).astype(BF16)


def ffn_in(x, pair_w):
    rows, depth = x.shape
    columns = pair_w.shape[1] // 2
    steps = columns // TILE
    tile = pl.BlockSpec((rows, TILE), lambda i: (0, i))
    return pl.pallas_call(
        ffn_in_kernel,
        grid=(steps,),
        in_specs=[
            pl.BlockSpec((rows, depth), lambda i: (0, 0), pipeline_mode=pl.Buffered(1)),
            pl.BlockSpec((depth, TILE), lambda i: (0, i)),
            pl.BlockSpec((depth, TILE), lambda i: (0, i + steps)),
        ],
        out_specs=[tile] * 3,
        out_shape=[jax.ShapeDtypeStruct((rows, columns), t) for t in (F32, F32, BF16)],
        compiler_params=pltpu.CompilerParams(vmem_limit_bytes=VMEM_LIMIT),
        cost_estimate=pl.CostEstimate(flops=4 * rows * depth * columns, bytes_accessed=4 * depth * columns, transcendentals=0),
        name="ffn_in",
    )(x, pair_w, pair_w)


def ffn_back_kernel(x_ref, gate_ref, up_ref, w_ref, dgate_ref, dup_ref):
    dmid = dot(x_ref[...], w_ref[...])
    gate_pre, up_pre = gate_ref[...], up_ref[...]
    square = gate_pre * gate_pre
    bend = jnp.tanh(GELU * (gate_pre + CUBIC * square * gate_pre))
    slope = 0.5 * (1.0 + bend) + 0.5 * gate_pre * (1.0 - bend * bend) * GELU * (1.0 + 3 * CUBIC * square)
    dgate_ref[...] = (dmid * up_pre * slope).astype(BF16)
    dup_ref[...] = (dmid * (0.5 * gate_pre * (1.0 + bend))).astype(BF16)


def ffn_back(x, gate_pre, up_pre, down_t):
    rows, depth = x.shape
    columns = down_t.shape[1]
    tile = pl.BlockSpec((rows, TILE), lambda i: (0, i))
    return pl.pallas_call(
        ffn_back_kernel,
        grid=(columns // TILE,),
        in_specs=[
            pl.BlockSpec((rows, depth), lambda i: (0, 0), pipeline_mode=pl.Buffered(1)),
            tile,
            tile,
            pl.BlockSpec((depth, TILE), lambda i: (0, i)),
        ],
        out_specs=[tile] * 2,
        out_shape=[jax.ShapeDtypeStruct((rows, columns), BF16)] * 2,
        compiler_params=pltpu.CompilerParams(vmem_limit_bytes=VMEM_LIMIT),
        cost_estimate=pl.CostEstimate(flops=2 * rows * depth * columns, bytes_accessed=2 * depth * columns, transcendentals=0),
        name="ffn_back",
    )(x, gate_pre, up_pre, down_t)


def rows_kernel(terms, *refs):
    xs, w_ref, out_ref = refs[:terms], refs[terms], refs[terms + 1]
    depth = xs[0].shape[1]
    total = 0.0
    for m in range(terms):
        total = total + dot_back(xs[m][...], w_ref[:, m * depth : (m + 1) * depth])
    out_ref[...] = total.astype(BF16)


def rows_call(xs, w, name):
    rows, depth = xs[0].shape
    width, terms = w.shape[0], len(xs)
    return pl.pallas_call(
        functools.partial(rows_kernel, terms),
        grid=(width // TILE,),
        in_specs=[pl.BlockSpec((rows, depth), lambda i: (0, 0), pipeline_mode=pl.Buffered(1))] * terms
        + [pl.BlockSpec((TILE, terms * depth), lambda i: (i, 0))],
        out_specs=pl.BlockSpec((rows, TILE), lambda i: (0, i)),
        out_shape=jax.ShapeDtypeStruct((rows, width), BF16),
        compiler_params=pltpu.CompilerParams(vmem_limit_bytes=VMEM_LIMIT),
        cost_estimate=pl.CostEstimate(
            flops=2 * rows * depth * width * terms, bytes_accessed=2 * depth * width * terms, transcendentals=0
        ),
        name=name,
    )(*xs, w)


def visible_lists(block_mask, block_seq, block_place, per_device):
    tp = lax.axis_size("tp")
    ctx = lax.axis_index("ctx")
    total = block_seq.shape[0]
    owner = owners()
    of_group = tp * per_device
    inner = jnp.arange(of_group, dtype=jnp.int32)
    query_ids = ctx * of_group + inner
    key_ids = (owner[:, None] * of_group + inner[None, :]).reshape(-1)
    every = jnp.arange(total, dtype=jnp.int32)

    def look_up(ids, table):
        return jnp.sum(jnp.where(ids[:, None] == every[None, :], table[None, :], 0), axis=1)

    places = jnp.arange(block_mask.shape[0], dtype=jnp.int32)
    query_pick = (look_up(query_ids, block_place)[:, None] == places[None, :]).astype(F32)
    key_pick = (look_up(key_ids, block_place)[:, None] == places[None, :]).astype(F32)
    hits = dot_back(dot(query_pick, block_mask.astype(F32)), key_pick)
    same = look_up(query_ids, block_seq)[:, None] == look_up(key_ids, block_seq)[None, :]
    seen = (hits > 0.5) & same
    before = (every[:, None] < every[None, :]).astype(F32)
    rank = dot(seen.astype(F32), before).astype(jnp.int32)
    wanted = seen[:, None, :] & (rank[:, None, :] == every[None, :, None])
    index = jnp.sum(jnp.where(wanted, every[None, None, :], 0), axis=2)
    index = jnp.pad(index, ((0, 0), (0, KEY_STEP)))
    return index, jnp.sum(seen.astype(jnp.int32), axis=1)


def gather_small(x):
    size = lax.axis_size("ctx")
    orders = outer_bits(0), outer_bits(1)
    held = {(0,) * steps_of_hops(): x}
    rows = x.shape[0]

    def send(pairs):
        came = lax.ppermute(jnp.concatenate(list(held.values()), axis=0), "ctx", pairs)
        return {t: came[n * rows : (n + 1) * rows] for n, t in enumerate(held)}

    for s in range(steps_of_hops()):
        came = send([(i, i ^ (1 << orders[i % 2][s])) for i in range(size)])
        held |= {flipped(t, s, 1): v for t, v in came.items()}
    other = {t[::-1]: v for t, v in send([(i, i ^ 1) for i in range(size)]).items()}
    blocks = jnp.stack([half[t] for half in (held, other) for t in places()])
    spots = []
    for j in range(size):
        found = [jnp.where(owner_at(p) == j, p, 0) for p in range(size)]
        spots.append(functools.reduce(jnp.add, found))
    return jnp.concatenate([lax.dynamic_index_in_dim(blocks, at, 0, keepdims=False) for at in spots], axis=1)


def sum_gains(terms):
    size, tp, me = lax.axis_size("ctx"), lax.axis_size("tp"), lax.axis_index("tp")
    orders = outer_bits(0), outer_bits(1)
    rows, width = terms.shape
    chunk, half = width // size, size // 2
    spots = places()
    parts = [lax.dynamic_slice_in_dim(terms, owner_at(p) * chunk, chunk, 1) for p in range(size)]

    def send(values, pairs):
        came = lax.ppermute(jnp.concatenate(values, axis=0), "ctx", pairs)
        return [came[n * rows : (n + 1) * rows] for n in range(len(values))]

    came = send(parts[half:], [(i, i ^ 1) for i in range(size)])
    now = {t: parts[n] + came[spots.index(t[::-1])] for n, t in enumerate(spots)}
    for s in range(steps_of_hops()):
        gone = [t for t in now if t[s]]
        came = send([now[t] for t in gone], [(i, i ^ (1 << orders[i % 2][s])) for i in range(size)])
        came = {flipped(t, s, 0): v for t, v in zip(gone, came)}
        now = {t: v + came[t] for t, v in now.items() if not t[s]}
    (mine,) = now.values()
    per = rows // tp

    def rows_of(shift):
        return lax.dynamic_slice_in_dim(mine, ((me + shift) % tp) * per, per, 0)

    total = rows_of(0)
    for shift in range(1, tp):
        total = total + lax.ppermute(rows_of(shift), "tp", [(i, (i + shift) % tp) for i in range(tp)])
    return total


def on_device(
    tokens,
    cotangent,
    w_query,
    key_projection,
    value_projection,
    w_out,
    w_gate,
    w_up,
    w_down,
    norm_gains,
    block_mask,
    block_seq,
    block_place,
):
    per_device = tokens.shape[0] // BLOCK_TOKENS
    scale = HEAD_SIZE ** (-0.5)
    q_cols, kv_cols = w_query.shape[1], key_projection.shape[1]
    in_cols = q_cols + 2 * kv_cols
    lanes = Lanes()

    def gather_weight(w):
        return lax.all_gather(w, "ctx", axis=0, tiled=True)

    wide = gather_weight(jnp.concatenate([w_query, key_projection, value_projection, w_out.T], axis=1))
    gains = gather_small(norm_gains)
    cot = cotangent.astype(F32)
    index, count = visible_lists(block_mask, block_seq, block_place, per_device)

    rows_in = gather_line(tokens)
    pair_w = gather_weight(tie_all(jnp.concatenate([w_gate, w_up], axis=1), [wide, rows_in, gains]))
    gains = 1.0 + gains.astype(F32)
    half = wide.shape[0] // 2
    core = lax.axis_index("ctx") % 2
    out_half = lax.dynamic_slice_in_dim(wide, core * half, half, 0)[:, in_cols:]
    out_steps, inner_steps = [], []
    wide = wide[:, :in_cols]
    rows_in = rows_in.astype(F32)
    normed = (rows_in * inv_rms(rows_in) * gains[0]).astype(BF16)
    qkv = dot(normed, wide)
    q = (qkv[:, :q_cols] * scale).astype(BF16)
    kv_own = qkv[:, q_cols:].astype(BF16)
    out_half = gather_line(tie(out_half, rows_in), axis=1, steps=out_steps)
    kv = tie_all(Gather(lanes, kv_own).rows(), out_steps[0])

    outcome, totals = attend(index, count, q, kv)
    attended = tie_all(outcome.astype(BF16), out_steps[1])
    rows = tokens.shape[0]
    own_heads = exchange_tp(lambda i: lax.dynamic_slice_in_dim(attended, i * rows, rows, 0), 1)
    out_other = lanes.near(tie(out_half, attended))
    out_t = jnp.zeros((2 * half, out_half.shape[1]), BF16)
    out_t = lax.dynamic_update_slice_in_dim(out_t, out_half, core * half, 0)
    out_t = lax.dynamic_update_slice_in_dim(out_t, out_other, (1 - core) * half, 0)
    branch = dot_back(own_heads, out_t)
    size = lax.axis_size("ctx")

    xf = tokens.astype(F32)
    s_branch = inv_rms(branch)
    hidden = xf + branch * s_branch * gains[1]
    s_hidden = inv_rms(hidden)
    inner = gather_line((hidden * s_hidden * gains[2]).astype(BF16), steps=inner_steps)
    down_t = gather_weight(tie_all(w_down.T, [pair_w] + inner_steps[0]))
    gate_pre, up_pre, mid = ffn_in(inner, pair_w)
    feed = scatter_tp(rows_call([mid], down_t, "ffn_out"))
    s_feed = inv_rms(feed)
    mixed = (hidden + feed * s_feed * gains[3]).astype(BF16)
    term_four = jnp.sum(cot * feed * s_feed, axis=0)
    dfeed = gather_tp(norm_input_grad(feed, s_feed, gains[3], cot).astype(BF16))

    down = scatter_grad(lanes, dfeed, mid)
    dgate, dup = ffn_back(dfeed, gate_pre, up_pre, down_t)
    dinner_part = rows_call([tie(dgate, down.out), dup], pair_w, "ffn_back_in")
    down.hop()
    gate = scatter_grad(lanes, inner, tie(dgate, dinner_part), [down.came[0]])
    down.hop()
    gate.hop()
    dinner = tie_all(scatter_tp(dinner_part), [down.came[1], gate.out])
    down_sum = down.result()
    term_three = jnp.sum(dinner * hidden * s_hidden, axis=0)
    dhidden = cot + norm_input_grad(hidden, s_hidden, gains[2], dinner)
    term_two = jnp.sum(dhidden * branch * s_branch, axis=0)
    dbranch = norm_input_grad(branch, s_branch, gains[1], dhidden).astype(BF16)
    dheads = dot(dbranch, out_t).astype(BF16)
    head_cols = attended.shape[1]
    dattended = exchange_tp(lambda i: lax.dynamic_slice_in_dim(dheads, i * head_cols, head_cols, 1), 0)
    dattended = tie_all(dattended, [gate.came[0]])
    up_part = dot_rows(inner, tie(dup, dheads)).astype(BF16)
    grad_up = lax.psum_scatter(up_part, "ctx", scatter_dimension=0, tiled=True).astype(F32)
    gate.hop([dheads])
    dbranch = gather_line(tie(dbranch, dattended))

    dq, dkv = attend_back(index, count, q, dattended, outcome, totals, kv)
    dq = dq * jnp.asarray(scale, BF16)
    dkv = tie_all(dkv, [gate.came[1]])
    dkv = dkv.reshape(2, size // 2, kv_own.shape[0], 2 * kv_cols)
    dkv_own = Scatter(lanes, dkv[1], dkv[0]).result().astype(BF16)
    grad_gate = gate.result()
    dqkv = jnp.concatenate([dq, dkv_own], axis=1)
    dnormed_part = tie(dot_back(dqkv, wide).astype(BF16), grad_up)
    rest = scatter_grads(lanes, [(tie(dbranch, dnormed_part), attended), (normed, tie(dqkv, dnormed_part))]).result()
    cuts = [0, attended.shape[1], attended.shape[1] + q_cols, attended.shape[1] + q_cols + kv_cols, rest.shape[1]]
    grad_out, grad_query, grad_key, grad_value = [rest[:, i:j] for i, j in zip(cuts, cuts[1:])]
    term_one = jnp.sum(dnormed_part.astype(F32) * rows_in * inv_rms(rows_in), axis=0)
    dnormed = tie_all(scatter_tp(dnormed_part), [])
    grad_gains = sum_gains(jnp.stack([term_one, term_two, term_three, term_four]))
    grad_tokens = dhidden + norm_input_grad(xf, inv_rms(xf), gains[0], dnormed)
    return (
        mixed,
        grad_tokens,
        grad_query,
        grad_key,
        grad_value,
        grad_out.T,
        grad_gate,
        grad_up,
        down_sum.T,
        grad_gains,
    )


def solution(mesh):
    rows, weight, turned = P(("ctx", "tp"), None), P("ctx", "tp"), P("tp", "ctx")
    in_specs = (rows, rows, weight, weight, weight, turned, weight, weight, turned, P(None, "ctx"), P(), P(), P())
    out_specs = (rows, rows, weight, weight, weight, turned, weight, weight, turned, turned)
    return jax.shard_map(on_device, mesh=mesh, in_specs=in_specs, out_specs=out_specs, check_vma=False)
```

```python
import functools
import itertools

import jax
import jax.numpy as jnp
from jax import lax
from jax.experimental import pallas as pl
from jax.experimental.pallas import tpu as pltpu
from jax.sharding import PartitionSpec as P

QUERY_HEADS = 8
KEY_VALUE_HEADS = 4
HEAD_SIZE = 256
SCORE_SOFT_LIMIT = 50
BLOCK_TOKENS = 128
EPSILON = 1e-06
KEY_STEP = 4

F32 = jnp.float32
BF16 = jnp.bfloat16


def dot(a, b):
    return jnp.dot(a, b, preferred_element_type=F32)


def dot_back(a, b):
    return lax.dot_general(a, b, (((1,), (1,)), ((), ())), preferred_element_type=F32)


def dot_rows(a, b):
    return lax.dot_general(a, b, (((0,), (0,)), ((), ())), preferred_element_type=F32)


def inv_rms(v):
    return lax.rsqrt(jnp.mean(v * v, axis=-1, keepdims=True) + EPSILON)


def norm_input_grad(v, s, gain, c):
    cw = c * gain
    return s * cw - v * (s * s * s) * jnp.mean(cw * v, axis=-1, keepdims=True)


def outer_bits(odd):
    size = lax.axis_size("ctx")
    bits = size.bit_length() - 1
    assert size == 1 << bits and bits >= 1
    order = list(range(bits - 1, 0, -1))
    return order[::-1] if odd else order


def steps_of_hops():
    return len(outer_bits(0))


def places():
    return list(itertools.product((0, 1), repeat=steps_of_hops()))


def flipped(t, s, value):
    return t[:s] + (value,) + t[s + 1 :]


def distances(odd):
    order = outer_bits(odd)
    return [c + sum(b << o for b, o in zip(t, order)) for c in (0, 1) for t in places()]


def owners():
    ctx = lax.axis_index("ctx")
    rel = jnp.where(ctx % 2 == 0, jnp.array(distances(0), jnp.int32), jnp.array(distances(1), jnp.int32))
    return ctx ^ rel


def tie(x, earlier):
    return lax.optimization_barrier((x, earlier))[0]


def tie_all(x, earlier):
    for e in earlier:
        x = tie(x, e)
    return x


def cut_rows(x, count):
    rows = x.shape[0] // count
    return [x[i * rows : (i + 1) * rows] for i in range(count)]


class Lanes:
    def __init__(self):
        self.sent = {"far": [], "near": []}
        self.depth = {"far": 2, "near": 1}

    def send(self, lane, x, pairs, after=()):
        done, depth = self.sent[lane], self.depth[lane]
        if len(done) >= depth:
            x = tie(x, done[-depth])
        x = tie_all(x, after)
        done.append(lax.ppermute(x, "ctx", pairs))
        return done[-1]

    def hop(self, x, s, after):
        orders = outer_bits(0), outer_bits(1)
        return self.send("far", x, [(i, i ^ (1 << orders[i % 2][s])) for i in range(lax.axis_size("ctx"))], after)

    def near(self, x):
        return self.send("near", x, [(i, i ^ 1) for i in range(lax.axis_size("ctx"))])


class Gather:
    def __init__(self, lanes, x):
        self.lanes, self.held, self.other = lanes, {(0,) * steps_of_hops(): x}, {}
        self.todo, self.after = self.plan(), ()

    def plan(self):
        held = self.held
        for s in range(steps_of_hops()):
            for t in list(held):
                held[flipped(t, s, 1)] = self.lanes.hop(held[t], s, self.after)
                self.after = ()
                yield

    def step(self, count=1, after=()):
        self.after = after
        for _ in range(count):
            next(self.todo, None)
        return self

    def pieces(self):
        for _ in self.todo:
            pass
        for t, v in self.held.items():
            self.other[t[::-1]] = self.lanes.near(v)
        return [half[t] for half in (self.held, self.other) for t in places()]

    def rows(self):
        return jnp.concatenate(self.pieces(), axis=0)


class Scatter:
    def __init__(self, lanes, sent, kept, after=()):
        self.lanes, self.came = lanes, []
        self.sent = sent
        lanes.depth = {"far": 1, "near": 4}
        self.got = [lanes.near(tie_all(v.astype(BF16), after)) for v in sent]
        spots = places()
        back = [spots.index(t[::-1]) for t in spots]
        pairs = [(kept[i], self.got[back[i]]) for i in range(len(spots))]
        self.now = {t: k.astype(F32) + g.astype(F32) for t, (k, g) in zip(spots, pairs)}
        self.pack()

    def pack(self):
        self.gone = [t for t in self.now if t[len(self.came)]]
        self.out = jnp.concatenate([self.now[t].astype(BF16) for t in self.gone], axis=0)

    def hop(self, after=()):
        s = len(self.came)
        came = self.lanes.hop(self.out, s, after)
        self.came.append(came)
        parts = dict(zip(self.gone, cut_rows(came, len(self.gone))))
        self.now = {t: v + parts[flipped(t, s, 1)].astype(F32) for t, v in self.now.items() if not t[s]}
        if s + 1 < steps_of_hops():
            self.pack()
        return self

    def result(self):
        while len(self.came) < steps_of_hops():
            self.hop()
        (value,) = self.now.values()
        return value


def owner_at(p):
    ctx = lax.axis_index("ctx")
    return ctx ^ jnp.where(ctx % 2 == 0, distances(0)[p], distances(1)[p])


def scatter_grads(lanes, pairs, after=()):
    size = lax.axis_size("ctx")
    parts = [dot_rows(left, right).astype(BF16) for left, right in pairs]
    chunk = parts[0].shape[0] // size
    half = [owner_at(n) // 2 for n in range(size // 2)]
    core = lax.axis_index("ctx") % 2

    def chunks(side):
        found = []
        for at in half:
            cut = [lax.dynamic_slice_in_dim(part, (2 * at + side) * chunk, chunk, 0) for part in parts]
            found.append(cut[0] if len(cut) == 1 else jnp.concatenate(cut, axis=1))
        return found

    return Scatter(lanes, chunks(1 - core), chunks(core), after)


def scatter_grad(lanes, left, right, after=()):
    return scatter_grads(lanes, [(left, right)], after)


def gather_tp(x, axis=0):
    return lax.all_gather(x, "tp", axis=axis, tiled=True)


def scatter_tp(part):
    return lax.psum_scatter(part.astype(BF16), "tp", scatter_dimension=0, tiled=True).astype(F32)


def gather_line(x, axis=0, steps=None, after={}):
    size, me = lax.axis_size("tp"), lax.axis_index("tp")
    up, down = x, x
    ups, downs = {}, {}
    for s in range(1, size):
        up, down = [tie_all(v, after.get(s, ())) for v in (up, down)]
        up = lax.ppermute(up, "tp", [(i, i + 1) for i in range(s - 1, size - 1)])
        down = lax.ppermute(down, "tp", [(i, i - 1) for i in range(1, size - s + 1)])
        ups[s], downs[s] = up, down
        if steps is not None:
            steps.append([up, down])
    length = x.shape[axis]
    shape = x.shape[:axis] + (size * length,) + x.shape[axis + 1 :]
    out = lax.dynamic_update_slice_in_dim(jnp.zeros(shape, x.dtype), x, me * length, axis)
    for s in range(1, size):
        came = jnp.where(me >= s, ups[s], downs[size - s])
        out = lax.dynamic_update_slice_in_dim(out, came, (me - s + size) % size * length, axis)
    return out


def exchange_tp(take, axis):
    size, me = lax.axis_size("tp"), lax.axis_index("tp")
    came = [take(me)] + [None] * (size - 1)
    for r in sorted(range(1, size), key=lambda r: -min(r, size - r)):
        came[size - r] = lax.ppermute(take((me + r) % size), "tp", [(i, (i + r) % size) for i in range(size)])
    length = came[0].shape[axis]
    turned = jnp.concatenate(came + came[:-1], axis=axis)
    return lax.dynamic_slice_in_dim(turned, (size - me) % size * length, size * length, axis)


def take_blocks(ref, index_ref, query_block, step, blocks):
    places = [index_ref[query_block, step * KEY_STEP + j] for j in range(KEY_STEP)]
    starts = [pl.multiple_of(p * BLOCK_TOKENS, BLOCK_TOKENS) for p in places]
    return starts, jnp.concatenate([ref[pl.ds(s, BLOCK_TOKENS), :] for s in starts], axis=0)


def stack_heads(x):
    heads = x.shape[1] // HEAD_SIZE
    return jnp.concatenate([x[:, h * HEAD_SIZE : (h + 1) * HEAD_SIZE] for h in range(heads)], axis=0)


def unstack_heads(x):
    rows = BLOCK_TOKENS
    return jnp.concatenate([x[h * rows : (h + 1) * rows] for h in range(x.shape[0] // rows)], axis=1)


def attend_kernel(index_ref, count_ref, q_ref, k_ref, v_ref, out_ref, total_ref, acc_ref):
    i = pl.program_id(0)
    count = count_ref[i]
    q = stack_heads(q_ref[...])
    acc_ref[...] = jnp.zeros_like(acc_ref)
    total_ref[...] = jnp.zeros_like(total_ref)

    def body(step, carry):
        starts, keys = take_blocks(k_ref, index_ref, i, step, KEY_STEP)
        values = jnp.concatenate([v_ref[pl.ds(s, BLOCK_TOKENS), :] for s in starts], axis=0)
        scores = dot_back(q, keys)
        grown = jnp.exp(SCORE_SOFT_LIMIT * jnp.tanh(scores * (1.0 / SCORE_SOFT_LIMIT)))
        pieces = []
        for j in range(KEY_STEP):
            seen = (step * KEY_STEP + j) < count
            piece = grown[:, j * BLOCK_TOKENS : (j + 1) * BLOCK_TOKENS]
            pieces.append(jnp.where(seen, piece, 0.0))
        total_ref[...] += functools.reduce(jnp.add, pieces)
        acc_ref[...] += dot(jnp.concatenate(pieces, axis=1).astype(BF16), values)
        return carry

    lax.fori_loop(0, (count + KEY_STEP - 1) // KEY_STEP, body, 0)
    totals = jnp.sum(total_ref[...], axis=1, keepdims=True)
    total_ref[...] = jnp.broadcast_to(totals, total_ref.shape)
    out_ref[...] = unstack_heads(acc_ref[...] / totals)


def attend_back_kernel(
    index_ref, count_ref, q_ref, dout_ref, out_ref, total_ref, k_ref, v_ref, dq_ref, dkv_ref, acc_ref
):
    i = pl.program_id(0)

    @pl.when(i == 0)
    def _():
        dkv_ref[...] = jnp.zeros_like(dkv_ref)

    count = count_ref[i]
    q = stack_heads(q_ref[...])
    dout = stack_heads(dout_ref[...]).astype(F32)
    inverse = 1.0 / total_ref[:, :1]
    scaled = (dout * inverse).astype(BF16)
    weighted = dout * stack_heads(out_ref[...]) * inverse
    ones = jnp.ones((8, HEAD_SIZE), F32)
    dtotal = -lax.dot_general(
        ones, weighted, (((1,), (1,)), ((), ())), precision=lax.Precision.HIGHEST, preferred_element_type=F32
    )[:1]
    acc_ref[...] = jnp.zeros_like(acc_ref)

    def body(step, carry):
        starts, keys = take_blocks(k_ref, index_ref, i, step, KEY_STEP)
        values = jnp.concatenate([v_ref[pl.ds(s, BLOCK_TOKENS), :] for s in starts], axis=0)
        soft = jnp.tanh(dot_back(keys, q) * (1.0 / SCORE_SOFT_LIMIT))
        grown = jnp.exp(SCORE_SOFT_LIMIT * soft)
        pieces = []
        for j in range(KEY_STEP):
            seen = (step * KEY_STEP + j) < count
            piece = grown[j * BLOCK_TOKENS : (j + 1) * BLOCK_TOKENS]
            pieces.append(jnp.where(seen, piece, 0.0))
        grown = jnp.concatenate(pieces, axis=0)
        dprob = dot_back(values, scaled)
        dscores = (grown * (dprob + dtotal) * (1.0 - soft * soft)).astype(BF16)
        acc_ref[...] += dot_rows(dscores, keys)
        dkeys = dot(dscores, q)
        dvalues = dot(grown.astype(BF16), scaled)
        for j in range(KEY_STEP):
            at = pl.ds(starts[j], BLOCK_TOKENS)
            dkv_ref[at, :HEAD_SIZE] += dkeys[j * BLOCK_TOKENS : (j + 1) * BLOCK_TOKENS]
            dkv_ref[at, HEAD_SIZE:] += dvalues[j * BLOCK_TOKENS : (j + 1) * BLOCK_TOKENS]
        return carry

    lax.fori_loop(0, (count + KEY_STEP - 1) // KEY_STEP, body, 0)
    dq_ref[...] = unstack_heads(acc_ref[...]).astype(BF16)


VMEM_LIMIT = 56 * 1024 * 1024


def whole_spec(rows, columns, at=0):
    return pl.BlockSpec((rows, columns), lambda i, *_: (0, at), pipeline_mode=pl.Buffered(1))


def row_spec(rows, columns):
    return pl.BlockSpec((rows, columns), lambda i, *_: (i, 0))


def attend(index, count, q, kv):
    rows, columns = q.shape
    blocks, stacked = rows // BLOCK_TOKENS, BLOCK_TOKENS * (columns // HEAD_SIZE)
    return pl.pallas_call(
        attend_kernel,
        grid_spec=pltpu.PrefetchScalarGridSpec(
            num_scalar_prefetch=2,
            grid=(blocks,),
            in_specs=[row_spec(BLOCK_TOKENS, columns), whole_spec(kv.shape[0], HEAD_SIZE), whole_spec(kv.shape[0], HEAD_SIZE, 1)],
            out_specs=[row_spec(BLOCK_TOKENS, columns), row_spec(stacked, BLOCK_TOKENS)],
            scratch_shapes=[pltpu.VMEM((stacked, HEAD_SIZE), F32)],
        ),
        out_shape=[
            jax.ShapeDtypeStruct((rows, columns), F32),
            jax.ShapeDtypeStruct((blocks * stacked, BLOCK_TOKENS), F32),
        ],
        compiler_params=pltpu.CompilerParams(vmem_limit_bytes=VMEM_LIMIT),
        cost_estimate=pl.CostEstimate(flops=2 * rows * columns * kv.shape[0], bytes_accessed=6 << 20, transcendentals=0),
    )(index, count, q, kv, kv)


def attend_back(index, count, q, dout, out, totals, kv):
    rows, columns = q.shape
    blocks, stacked = rows // BLOCK_TOKENS, BLOCK_TOKENS * (columns // HEAD_SIZE)
    row = row_spec(BLOCK_TOKENS, columns)
    return pl.pallas_call(
        attend_back_kernel,
        grid_spec=pltpu.PrefetchScalarGridSpec(
            num_scalar_prefetch=2,
            grid=(blocks,),
            in_specs=[row, row, row, row_spec(stacked, BLOCK_TOKENS)]
            + [whole_spec(kv.shape[0], HEAD_SIZE), whole_spec(kv.shape[0], HEAD_SIZE, 1)],
            out_specs=[row, whole_spec(*kv.shape)],
            scratch_shapes=[pltpu.VMEM((stacked, HEAD_SIZE), F32)],
        ),
        out_shape=[
            jax.ShapeDtypeStruct((rows, columns), BF16),
            jax.ShapeDtypeStruct(kv.shape, F32),
        ],
        compiler_params=pltpu.CompilerParams(vmem_limit_bytes=VMEM_LIMIT),
        cost_estimate=pl.CostEstimate(flops=5 * rows * columns * kv.shape[0], bytes_accessed=16 << 20, transcendentals=0),
    )(index, count, q, dout, out, totals, kv, kv)


GELU = 0.7978845608028654
CUBIC = 0.044715
TILE = 768
PAIR_TILE = 256


def ffn_in_kernel(x_ref, gate_w_ref, up_w_ref, gate_ref, up_ref, mid_ref):
    x = x_ref[...]
    gate_pre = dot(x, gate_w_ref[...])
    up_pre = dot(x, up_w_ref[...])
    bend = jnp.tanh(GELU * (gate_pre + CUBIC * gate_pre * gate_pre * gate_pre))
    gate_ref[...] = gate_pre
    up_ref[...] = up_pre
    mid_ref[...] = (0.5 * gate_pre * (1.0 + bend) * up_pre).astype(BF16)


def ffn_in(x, pair_w):
    rows, depth = x.shape
    columns = pair_w.shape[1] // 2
    steps = columns // TILE
    tile = pl.BlockSpec((rows, TILE), lambda i: (0, i))
    return pl.pallas_call(
        ffn_in_kernel,
        grid=(steps,),
        in_specs=[
            pl.BlockSpec((rows, depth), lambda i: (0, 0), pipeline_mode=pl.Buffered(1)),
            pl.BlockSpec((depth, TILE), lambda i: (0, i)),
            pl.BlockSpec((depth, TILE), lambda i: (0, i + steps)),
        ],
        out_specs=[tile] * 3,
        out_shape=[jax.ShapeDtypeStruct((rows, columns), t) for t in (F32, F32, BF16)],
        compiler_params=pltpu.CompilerParams(vmem_limit_bytes=VMEM_LIMIT),
        cost_estimate=pl.CostEstimate(flops=4 * rows * depth * columns, bytes_accessed=4 * depth * columns, transcendentals=0),
        name="ffn_in",
    )(x, pair_w, pair_w)


def ffn_back_kernel(x_ref, gate_ref, up_ref, w_ref, dgate_ref, dup_ref):
    dmid = dot(x_ref[...], w_ref[...])
    gate_pre, up_pre = gate_ref[...], up_ref[...]
    square = gate_pre * gate_pre
    bend = jnp.tanh(GELU * (gate_pre + CUBIC * square * gate_pre))
    slope = 0.5 * (1.0 + bend) + 0.5 * gate_pre * (1.0 - bend * bend) * GELU * (1.0 + 3 * CUBIC * square)
    dgate_ref[...] = (dmid * up_pre * slope).astype(BF16)
    dup_ref[...] = (dmid * (0.5 * gate_pre * (1.0 + bend))).astype(BF16)


def ffn_back(x, gate_pre, up_pre, down_t):
    rows, depth = x.shape
    columns = down_t.shape[1]
    tile = pl.BlockSpec((rows, TILE), lambda i: (0, i))
    return pl.pallas_call(
        ffn_back_kernel,
        grid=(columns // TILE,),
        in_specs=[
            pl.BlockSpec((rows, depth), lambda i: (0, 0), pipeline_mode=pl.Buffered(1)),
            tile,
            tile,
            pl.BlockSpec((depth, TILE), lambda i: (0, i)),
        ],
        out_specs=[tile] * 2,
        out_shape=[jax.ShapeDtypeStruct((rows, columns), BF16)] * 2,
        compiler_params=pltpu.CompilerParams(vmem_limit_bytes=VMEM_LIMIT),
        cost_estimate=pl.CostEstimate(flops=2 * rows * depth * columns, bytes_accessed=2 * depth * columns, transcendentals=0),
        name="ffn_back",
    )(x, gate_pre, up_pre, down_t)


def rows_kernel(terms, *refs):
    xs, w_ref, out_ref = refs[:terms], refs[terms], refs[terms + 1]
    depth = xs[0].shape[1]
    total = 0.0
    for m in range(terms):
        total = total + dot_back(xs[m][...], w_ref[:, m * depth : (m + 1) * depth])
    out_ref[...] = total.astype(BF16)


def rows_call(xs, w, name):
    rows, depth = xs[0].shape
    width, terms = w.shape[0], len(xs)
    tile = TILE if terms == 1 else PAIR_TILE
    return pl.pallas_call(
        functools.partial(rows_kernel, terms),
        grid=(width // tile,),
        in_specs=[pl.BlockSpec((rows, depth), lambda i: (0, 0), pipeline_mode=pl.Buffered(1))] * terms
        + [pl.BlockSpec((tile, terms * depth), lambda i: (i, 0))],
        out_specs=pl.BlockSpec((rows, tile), lambda i: (0, i)),
        out_shape=jax.ShapeDtypeStruct((rows, width), BF16),
        compiler_params=pltpu.CompilerParams(vmem_limit_bytes=VMEM_LIMIT),
        cost_estimate=pl.CostEstimate(
            flops=2 * rows * depth * width * terms, bytes_accessed=2 * depth * width * terms, transcendentals=0
        ),
        name=name,
    )(*xs, w)


def visible_lists(block_mask, block_seq, block_place, per_device):
    tp = lax.axis_size("tp")
    ctx = lax.axis_index("ctx")
    total = block_seq.shape[0]
    owner = owners()
    of_group = tp * per_device
    inner = jnp.arange(of_group, dtype=jnp.int32)
    query_ids = ctx * of_group + inner
    key_ids = (owner[:, None] * of_group + inner[None, :]).reshape(-1)
    every = jnp.arange(total, dtype=jnp.int32)

    def look_up(ids, table):
        return jnp.sum(jnp.where(ids[:, None] == every[None, :], table[None, :], 0), axis=1)

    places = jnp.arange(block_mask.shape[0], dtype=jnp.int32)
    query_pick = (look_up(query_ids, block_place)[:, None] == places[None, :]).astype(F32)
    key_pick = (look_up(key_ids, block_place)[:, None] == places[None, :]).astype(F32)
    hits = dot_back(dot(query_pick, block_mask.astype(F32)), key_pick)
    same = look_up(query_ids, block_seq)[:, None] == look_up(key_ids, block_seq)[None, :]
    seen = (hits > 0.5) & same
    before = (every[:, None] < every[None, :]).astype(F32)
    rank = dot(seen.astype(F32), before).astype(jnp.int32)
    wanted = seen[:, None, :] & (rank[:, None, :] == every[None, :, None])
    index = jnp.sum(jnp.where(wanted, every[None, None, :], 0), axis=2)
    index = jnp.pad(index, ((0, 0), (0, KEY_STEP)))
    return index, jnp.sum(seen.astype(jnp.int32), axis=1)


def gather_small(x):
    size = lax.axis_size("ctx")
    orders = outer_bits(0), outer_bits(1)
    held = {(0,) * steps_of_hops(): x}
    rows = x.shape[0]

    def send(pairs):
        came = lax.ppermute(jnp.concatenate(list(held.values()), axis=0), "ctx", pairs)
        return {t: came[n * rows : (n + 1) * rows] for n, t in enumerate(held)}

    for s in range(steps_of_hops()):
        came = send([(i, i ^ (1 << orders[i % 2][s])) for i in range(size)])
        held |= {flipped(t, s, 1): v for t, v in came.items()}
    other = {t[::-1]: v for t, v in send([(i, i ^ 1) for i in range(size)]).items()}
    blocks = jnp.stack([half[t] for half in (held, other) for t in places()])
    spots = []
    for j in range(size):
        found = [jnp.where(owner_at(p) == j, p, 0) for p in range(size)]
        spots.append(functools.reduce(jnp.add, found))
    return jnp.concatenate([lax.dynamic_index_in_dim(blocks, at, 0, keepdims=False) for at in spots], axis=1)


def sum_gains(terms):
    size, tp, me = lax.axis_size("ctx"), lax.axis_size("tp"), lax.axis_index("tp")
    orders = outer_bits(0), outer_bits(1)
    rows, width = terms.shape
    chunk, half = width // size, size // 2
    spots = places()
    parts = [lax.dynamic_slice_in_dim(terms, owner_at(p) * chunk, chunk, 1) for p in range(size)]

    def send(values, pairs):
        came = lax.ppermute(jnp.concatenate(values, axis=0), "ctx", pairs)
        return [came[n * rows : (n + 1) * rows] for n in range(len(values))]

    came = send(parts[half:], [(i, i ^ 1) for i in range(size)])
    now = {t: parts[n] + came[spots.index(t[::-1])] for n, t in enumerate(spots)}
    for s in range(steps_of_hops()):
        gone = [t for t in now if t[s]]
        came = send([now[t] for t in gone], [(i, i ^ (1 << orders[i % 2][s])) for i in range(size)])
        came = {flipped(t, s, 0): v for t, v in zip(gone, came)}
        now = {t: v + came[t] for t, v in now.items() if not t[s]}
    (mine,) = now.values()
    per = rows // tp

    def rows_of(shift):
        return lax.dynamic_slice_in_dim(mine, ((me + shift) % tp) * per, per, 0)

    total = rows_of(0)
    for shift in range(1, tp):
        total = total + lax.ppermute(rows_of(shift), "tp", [(i, (i + shift) % tp) for i in range(tp)])
    return total


def on_device(
    tokens,
    cotangent,
    w_query,
    key_projection,
    value_projection,
    w_out,
    w_gate,
    w_up,
    w_down,
    norm_gains,
    block_mask,
    block_seq,
    block_place,
):
    per_device = tokens.shape[0] // BLOCK_TOKENS
    scale = HEAD_SIZE ** (-0.5)
    q_cols, kv_cols = w_query.shape[1], key_projection.shape[1]
    in_cols = q_cols + 2 * kv_cols
    lanes = Lanes()

    def gather_weight(w):
        return lax.all_gather(w, "ctx", axis=0, tiled=True)

    wide = gather_weight(jnp.concatenate([w_query, key_projection, value_projection, w_out.T], axis=1))
    gains = gather_small(norm_gains)
    cot = cotangent.astype(F32)
    index, count = visible_lists(block_mask, block_seq, block_place, per_device)

    rows_in = gather_line(tokens)
    pair_w = gather_weight(tie_all(jnp.concatenate([w_gate, w_up], axis=1), [wide, rows_in, gains]))
    gains = 1.0 + gains.astype(F32)
    half = wide.shape[0] // 2
    core = lax.axis_index("ctx") % 2
    out_half = lax.dynamic_slice_in_dim(wide, core * half, half, 0)[:, in_cols:]
    out_steps, inner_steps = [], []
    wide = wide[:, :in_cols]
    rows_in = rows_in.astype(F32)
    normed = (rows_in * inv_rms(rows_in) * gains[0]).astype(BF16)
    qkv = dot(normed, wide)
    q = (qkv[:, :q_cols] * scale).astype(BF16)
    kv_own = qkv[:, q_cols:].astype(BF16)
    out_half = gather_line(tie(out_half, rows_in), axis=1, steps=out_steps)
    kv = tie_all(Gather(lanes, kv_own).rows(), out_steps[0])

    outcome, totals = attend(index, count, q, kv)
    attended = tie_all(outcome.astype(BF16), out_steps[1])
    rows = tokens.shape[0]
    own_heads = exchange_tp(lambda i: lax.dynamic_slice_in_dim(attended, i * rows, rows, 0), 1)
    out_other = lanes.near(tie(out_half, attended))
    out_t = jnp.zeros((2 * half, out_half.shape[1]), BF16)
    out_t = lax.dynamic_update_slice_in_dim(out_t, out_half, core * half, 0)
    out_t = lax.dynamic_update_slice_in_dim(out_t, out_other, (1 - core) * half, 0)
    branch = dot_back(own_heads, out_t)
    size = lax.axis_size("ctx")

    xf = tokens.astype(F32)
    s_branch = inv_rms(branch)
    hidden = xf + branch * s_branch * gains[1]
    s_hidden = inv_rms(hidden)
    inner = gather_line((hidden * s_hidden * gains[2]).astype(BF16), steps=inner_steps)
    down_t = gather_weight(tie_all(w_down.T, [pair_w, branch]))
    gate_pre, up_pre, mid = ffn_in(inner, pair_w)
    feed = scatter_tp(rows_call([mid], down_t, "ffn_out"))
    s_feed = inv_rms(feed)
    mixed = (hidden + feed * s_feed * gains[3]).astype(BF16)
    term_four = jnp.sum(cot * feed * s_feed, axis=0)
    dfeed = gather_tp(norm_input_grad(feed, s_feed, gains[3], cot).astype(BF16))

    down = scatter_grad(lanes, dfeed, mid)
    dgate, dup = ffn_back(dfeed, gate_pre, up_pre, down_t)
    dinner_part = rows_call([tie(dgate, down.out), dup], pair_w, "ffn_back_in")
    down.hop()
    gate = scatter_grad(lanes, inner, tie(dgate, dinner_part), [down.came[0]])
    down.hop()
    gate.hop()
    dinner = tie_all(scatter_tp(dinner_part), [down.came[1], gate.out])
    down_sum = down.result()
    term_three = jnp.sum(dinner * hidden * s_hidden, axis=0)
    dhidden = cot + norm_input_grad(hidden, s_hidden, gains[2], dinner)
    term_two = jnp.sum(dhidden * branch * s_branch, axis=0)
    dbranch = norm_input_grad(branch, s_branch, gains[1], dhidden).astype(BF16)
    dheads = dot(dbranch, out_t).astype(BF16)
    head_cols = attended.shape[1]
    dattended = exchange_tp(lambda i: lax.dynamic_slice_in_dim(dheads, i * head_cols, head_cols, 1), 0)
    dattended = tie_all(dattended, [gate.came[0]])
    up_part = dot_rows(inner, tie(dup, dheads)).astype(BF16)
    grad_up = lax.psum_scatter(up_part, "ctx", scatter_dimension=0, tiled=True).astype(F32)
    gate.hop([dheads])
    dbranch = gather_line(tie(dbranch, dattended))

    dq, dkv = attend_back(index, count, q, dattended, outcome, totals, kv)
    dq = dq * jnp.asarray(scale, BF16)
    dkv = tie_all(dkv, [gate.came[1]])
    dkv = dkv.reshape(2, size // 2, kv_own.shape[0], 2 * kv_cols)
    dkv_own = Scatter(lanes, dkv[1], dkv[0]).result().astype(BF16)
    grad_gate = gate.result()
    dqkv = jnp.concatenate([dq, dkv_own], axis=1)
    dnormed_part = tie(dot_back(dqkv, wide).astype(BF16), grad_up)
    rest = scatter_grads(lanes, [(tie(dbranch, dnormed_part), attended), (normed, tie(dqkv, dnormed_part))]).result()
    cuts = [0, attended.shape[1], attended.shape[1] + q_cols, attended.shape[1] + q_cols + kv_cols, rest.shape[1]]
    grad_out, grad_query, grad_key, grad_value = [rest[:, i:j] for i, j in zip(cuts, cuts[1:])]
    term_one = jnp.sum(dnormed_part.astype(F32) * rows_in * inv_rms(rows_in), axis=0)
    dnormed = tie_all(scatter_tp(dnormed_part), [])
    grad_gains = sum_gains(jnp.stack([term_one, term_two, term_three, term_four]))
    grad_tokens = dhidden + norm_input_grad(xf, inv_rms(xf), gains[0], dnormed)
    return (
        mixed,
        grad_tokens,
        grad_query,
        grad_key,
        grad_value,
        grad_out.T,
        grad_gate,
        grad_up,
        down_sum.T,
        grad_gains,
    )


def solution(mesh):
    rows, weight, turned = P(("ctx", "tp"), None), P("ctx", "tp"), P("tp", "ctx")
    in_specs = (rows, rows, weight, weight, weight, turned, weight, weight, turned, P(None, "ctx"), P(), P(), P())
    out_specs = (rows, rows, weight, weight, weight, turned, weight, weight, turned, turned)
    return jax.shard_map(on_device, mesh=mesh, in_specs=in_specs, out_specs=out_specs, check_vma=False)
```
